128 devices in a mesh: pipe: 4 (over z_hi, core), expert: 32 (over z_lo, x, y).
Axes of the slice: x: 4, y: 4, z: 4 (z_hi: 2, z_lo: 2; z = z_hi * 2 + z_lo), core: 2. Of those that a mesh axis runs over, the one named last changes fastest.
Arguments:
- out_grad: bfloat16 [32768, 7168], P(('pipe', 'expert')), may hold values from -0.29882812 to 0.29882812
- routes: int32 [32768, 1], P(('pipe', 'expert')), may hold values from 0 to 3; in each aligned block of 256 rows (0 to 255, 256 to 511, ...) at most 128 rows name the same one
- saved_hidden: bfloat16 [4, 32, 32, 128, 1024], P('pipe', 'expert'), may hold values from -6 to 6
- master: float32 [4, 32, 512, 896], P('pipe', 'expert'), may hold values from -4 to 4
- moment1: float32 [4, 32, 512, 896], P('pipe', 'expert'), may hold values from -3 to 3
- moment2: float32 [4, 32, 512, 896], P('pipe', 'expert'), may hold values from 0.05 to 4
Outputs:
- new_master: float32 [4, 32, 512, 896], P('pipe', 'expert')
- new_moment1: float32 [4, 32, 512, 896], P('pipe', 'expert')
- new_moment2: float32 [4, 32, 512, 896], P('pipe', 'expert')
The draws below stay inside these ranges and needn't reach their ends.
Inputs may be any that keep to these rules, and one draw needn't show every extreme that they name: `routes`: among the 256 slots of one device no expert is named more than 128 times; on some devices one expert is named exactly 128 times.
All inputs are finite; a program needn't handle non-finite values.
Results may differ from the reference program's by a relative error of at most 0.0003.
Values may be sent and summed in bfloat16 or wider, within the bound.
A program may use at most 128 MiB of HBM per device.

```python
import math
import jax
import jax.numpy as jnp
import numpy as np
from jax import lax

D = 7168
HID = 1024
EXPG = 4
SLOT_DEV = 256
CAP = 128
DS = 896
HALF = 512
SLOTS = 32768
N_PIPE = 4
N_EXPERT = 32


def levels(own_key, shape, pieces, low, top_value):
    def one(axis_at, blocks):
        steps = jax.random.uniform(jax.random.fold_in(jax.random.fold_in(own_key, 6), axis_at), (blocks,), jnp.float32, low / len(pieces), top_value / len(pieces))
        return jnp.repeat(jnp.exp(steps), shape[axis_at] // blocks).reshape((-1,) + (1,) * (len(shape) - axis_at - 1))

    level = one(*pieces[0])
    for cut in pieces[1:]:
        level = level * one(*cut)
    return level


def shared_out(key, own, number, rows, count, top, bound, skew):
    order = jax.random.permutation(key, count)
    packed, ordinary = shares(count, rows * top, bound, skew, True), shares(count, rows * top, bound, skew, False)
    places = jnp.arange(count)

    def named(lengths, turn):
        used = int((lengths > 0).sum())
        fixed = max(1, used // 4)
        shifted = fixed + (places - fixed + turn * (used - fixed)) % max(1, count - fixed)
        return jnp.zeros((count,), jnp.int32).at[order[jnp.where(places < fixed, places, shifted)]].set(jnp.asarray(lengths, jnp.int32))

    lengths = jnp.where(number % 4 == 0, named(packed, number // 4), named(ordinary, number - number // 4 - 1))
    mixed = jax.random.permutation(jax.random.fold_in(own, 3), count)
    source_of, taker = mixed[0:count // 2 * 2:2], mixed[1:count // 2 * 2:2]
    slack = jnp.minimum(lengths[source_of] - 1, bound - lengths[taker]) // 2
    slack = jnp.where((source_of == order[0]) | (taker == order[0]) | (lengths[taker] == 0), 0, jnp.maximum(slack, 0))
    shifted = jax.random.randint(jax.random.fold_in(own, 4), (count // 2,), 0, 1 << 20) % (slack + 1)
    lengths = lengths.at[source_of].add(-shifted).at[taker].add(shifted)
    members = jnp.searchsorted(jnp.cumsum(lengths), jnp.arange(rows * top), side="right").astype(jnp.int32)
    listing = members.reshape(top, rows).T
    listing = listing[jax.random.permutation(jax.random.fold_in(own, 1), rows)]
    turn = jax.random.randint(jax.random.fold_in(own, 2), (rows, 1), 0, top)
    return jnp.take_along_axis(listing, (jnp.arange(top)[None, :] + turn) % top, axis=1)


def shares(amount, total, most, slope, full):
    weights = [(1 << 20) // math.isqrt(rank ** slope) + 1 for rank in range(1, amount + 1)]
    largest = most if full else min(most, max(-(-total // amount), total * weights[0] // sum(weights)))
    least = 1 if total - largest >= amount - 1 else 0
    counts, spare = [largest] + [least] * (amount - 1), total - largest - least * (amount - 1)
    while spare > 0:
        movable = [i for i in range(1, amount) if counts[i] < largest] or [i for i in range(1, amount) if counts[i] < most]
        pool, left = sum([weights[i] for i in movable]), spare
        for i in movable:
            extra = min(most - counts[i], max(1, left * weights[i] // pool), spare)
            counts[i] = counts[i] + extra
            spare = spare - extra
    return np.array(counts)


def bell_draw(key, extent, scale, bound, cuts=(), held_as=jnp.bfloat16):
    factor_of = levels(key, extent, cuts, -0.22, 0.18) if cuts else 1.0
    drawn = jax.random.normal(key, extent, jnp.float32) * scale * factor_of
    return jnp.minimum(jnp.maximum(drawn, -bound), bound).astype(held_as)


def setup_inputs(seed: int = 0) -> dict:
    streams_of = jax.random.split(jax.random.key(seed), 7)
    out_grad = bell_draw(streams_of[0], (SLOTS, D), 0.05, 0.29882812, ((0, 128),))
    routes_keys = jax.random.split(jax.random.fold_in(streams_of[1], 1), SLOTS // SLOT_DEV)
    routes_turns = jax.random.permutation(jax.random.fold_in(streams_of[1], 3), SLOTS // SLOT_DEV)
    routes = jax.vmap(lambda own, number: shared_out(jax.random.fold_in(streams_of[1], 2), own, number, SLOT_DEV, EXPG, 1, CAP, 1))(routes_keys, routes_turns).reshape((SLOTS, 1))
    saved_hidden = bell_draw(streams_of[2], (N_PIPE, N_EXPERT, N_EXPERT, CAP, HID), 1.0, 6.0, ((0, 4), (1, 32)))
    master = bell_draw(streams_of[3], (N_PIPE, N_EXPERT, HALF, DS), 1.0, 4.0, ((0, 4), (1, 32)), jnp.float32)
    moment1 = bell_draw(streams_of[4], (N_PIPE, N_EXPERT, HALF, DS), 0.5, 3.0, ((0, 4), (1, 32)), jnp.float32)
    moment2 = jnp.clip(jnp.exp(math.log(4.0) - 4.3820266 * jax.random.uniform(streams_of[5], (N_PIPE, N_EXPERT, HALF, DS), jnp.float32) ** levels(streams_of[5], (N_PIPE, N_EXPERT, HALF, DS), ((0, 4), (1, 32)), -0.2, 0.2)), 0.05, 4.0)
    return {"out_grad": out_grad, "routes": routes, "saved_hidden": saved_hidden, "master": master, "moment1": moment1, "moment2": moment2}


def reference(out_grad, routes, saved_hidden, master, moment1, moment2):
    column_split = N_EXPERT // EXPG
    col_width = D // column_split
    all_grads = []
    for pipe_rank in range(N_PIPE):
        start_row = pipe_rank * N_EXPERT * SLOT_DEV
        rows_here = out_grad[start_row:start_row + N_EXPERT * SLOT_DEV].reshape(N_EXPERT, SLOT_DEV, D)
        route_ids = routes[start_row:start_row + N_EXPERT * SLOT_DEV, 0].reshape(N_EXPERT, SLOT_DEV)
        chosen = (route_ids[:, :, None] == jnp.arange(EXPG, dtype=jnp.int32)[None, None, :]).astype(jnp.int32)
        slot_rank = lax.optimization_barrier(jnp.sum((jnp.cumsum(chosen, axis=1) - chosen) * chosen, axis=2)).astype(jnp.int32)
        flat_slot = (route_ids * CAP + slot_rank).astype(jnp.int32)
        source_ids = jnp.broadcast_to(jnp.arange(N_EXPERT, dtype=jnp.int32)[:, None], flat_slot.shape)
        buffer = jnp.zeros((N_EXPERT, EXPG * CAP, D), jnp.bfloat16)
        buffer = buffer.at[source_ids, flat_slot].set(rows_here)
        buffer = buffer.reshape(N_EXPERT, EXPG, CAP, column_split, col_width)
        per_expert = []
        for expert_id in range(EXPG):
            received = buffer[:, expert_id].astype(jnp.float32)
            hidden_rows = saved_hidden[pipe_rank, expert_id * column_split:(expert_id + 1) * column_split].astype(jnp.float32)
            per_expert.append(jnp.einsum('jsch,scjw->jhw', hidden_rows, received, precision=lax.Precision.HIGHEST))
        all_grads.append(jnp.concatenate(per_expert, axis=0))
    grad_part = jnp.stack(all_grads, axis=0)
    summed = grad_part + grad_part[::-1]
    half_pipe = N_PIPE // 2
    gradient = jnp.concatenate([summed[:half_pipe, :, :HALF], summed[half_pipe:, :, HALF:]], axis=0)
    new_moment1 = 0.9 * moment1 + 0.1 * gradient
    new_moment2 = 0.95 * moment2 + 0.05 * gradient * gradient
    update = new_moment1 / (1.0 - 0.9 ** 10) / (jnp.sqrt(new_moment2 / (1.0 - 0.95 ** 10)) + 1e-08)
    new_master = master - 0.2 * (update + 0.05 * master)
    return (new_master, new_moment1, new_moment2)
```

```python
import functools

import jax
import jax.numpy as jnp
from jax import lax
from jax.experimental import pallas as pl
from jax.experimental.pallas import tpu as pltpu
from jax.sharding import PartitionSpec as P

EXPG = 4
LANE = 128
MESH = pl.DeviceIdType.MESH


def exchange_kernel(
    grad_hbm, routes_ref, hidden_hbm, total_hbm,
    grad, place, outbound, arrived, hidden, hidden_t, own, other, code, code_in, scale, scale_in, total,
    load_sem, local_sem, send_sem, recv_sem, code_send, code_recv, scale_send, scale_recv, store_sem,
):
    pipe, me = lax.axis_index("pipe"), lax.axis_index("expert")
    pipe_count, expert_count = lax.axis_size("pipe"), lax.axis_size("expert")
    chunks, _, cap, _ = outbound.shape
    slots, width = grad.shape
    split = expert_count // EXPG
    slab = width // split
    hid = hidden_t.shape[0]
    half = hid // 2
    mirror = pipe_count - 1 - pipe
    keep_high = pipe // (pipe_count // 2)
    own_start = pl.multiple_of(keep_high * half, half)
    other_start = pl.multiple_of((1 - keep_high) * half, half)
    tile = half // 2

    load_grad = pltpu.make_async_copy(grad_hbm, grad, load_sem.at[0])
    load_grad.start()
    load_hidden = pltpu.make_async_copy(hidden_hbm.at[0, 0], hidden, load_sem.at[1])
    load_hidden.start()

    barrier = pltpu.get_barrier_semaphore()

    def greet(step, carry):
        pl.semaphore_signal(
            barrier, inc=1, device_id=(pipe, lax.rem(me + step, expert_count)), device_id_type=MESH
        )
        return carry

    lax.fori_loop(1, expert_count, greet, 0)
    pl.semaphore_signal(barrier, inc=1, device_id=(mirror, me), device_id_type=MESH)

    route = routes_ref[...]
    chosen = jnp.broadcast_to(route, (8, slots)) == lax.broadcasted_iota(jnp.int32, (8, slots), 0)
    earlier = lax.broadcasted_iota(jnp.int32, (slots, slots), 0) < lax.broadcasted_iota(jnp.int32, (slots, slots), 1)
    before = jnp.dot(
        chosen.astype(jnp.bfloat16), earlier.astype(jnp.bfloat16), preferred_element_type=jnp.float32
    )
    rank = jnp.sum(jnp.where(chosen, before, 0.0), axis=0, keepdims=True).astype(jnp.int32)
    flat = jnp.broadcast_to(route * cap + rank, (EXPG * cap, slots))
    placed = flat == lax.broadcasted_iota(jnp.int32, (EXPG * cap, slots), 0)
    place[...] = placed.astype(jnp.bfloat16)

    load_grad.wait()

    def pick(chunk):
        def one(j, carry):
            start = pl.multiple_of(j * slab + chunk * LANE, LANE)
            picked = jnp.dot(place[...], grad[:, pl.ds(start, LANE)], preferred_element_type=jnp.float32)
            picked = picked.astype(jnp.bfloat16)
            for k in range(EXPG):
                outbound[chunk, k * split + j] = picked[k * cap:(k + 1) * cap]
            return carry

        lax.fori_loop(0, split, one, 0)

    def block(chunk, peer):
        return pltpu.make_async_remote_copy(
            src_ref=outbound.at[chunk, peer],
            dst_ref=arrived.at[chunk, me],
            send_sem=send_sem.at[chunk],
            recv_sem=recv_sem.at[chunk],
            device_id=(pipe, peer),
            device_id_type=MESH,
        )

    def local(chunk):
        return pltpu.make_async_copy(outbound.at[chunk, me], arrived.at[chunk, me], local_sem.at[chunk])

    def send(chunk):
        def one(step, carry):
            block(chunk, lax.rem(me + step, expert_count)).start()
            return carry

        lax.fori_loop(1, expert_count, one, 0)
        local(chunk).start()

    def all_blocks(chunk):
        others = pl.ds(0, expert_count - 1)
        return pltpu.make_async_remote_copy(
            src_ref=outbound.at[chunk, others],
            dst_ref=arrived.at[chunk, others],
            send_sem=send_sem.at[chunk],
            recv_sem=recv_sem.at[chunk],
            device_id=(pipe, me),
            device_id_type=MESH,
        )

    pick(0)
    pl.semaphore_wait(barrier, expert_count)
    send(0)

    def pick_send(chunk, carry):
        pick(chunk)
        send(chunk)
        return carry

    lax.fori_loop(1, chunks, pick_send, 0)

    load_hidden.wait()

    def turn(s, carry):
        at = pl.multiple_of(s * cap, cap)
        hidden_t[:, pl.ds(at, cap)] = hidden[s].T
        return carry

    lax.fori_loop(0, expert_count, turn, 0)

    def code_copy(chunk):
        return pltpu.make_async_remote_copy(
            src_ref=code.at[chunk], dst_ref=code_in.at[chunk],
            send_sem=code_send.at[chunk], recv_sem=code_recv.at[chunk],
            device_id=(mirror, me), device_id_type=MESH,
        )

    def scale_copy(chunk):
        return pltpu.make_async_remote_copy(
            src_ref=scale.at[chunk], dst_ref=scale_in.at[chunk],
            send_sem=scale_send.at[chunk], recv_sem=scale_recv.at[chunk],
            device_id=(mirror, me), device_id_type=MESH,
        )

    def store(chunk):
        start = pl.multiple_of(chunk * LANE, LANE)
        return pltpu.make_async_copy(total.at[chunk], total_hbm.at[:, pl.ds(start, LANE)], store_sem.at[chunk])

    def multiply(chunk, first, into):
        def one(i, carry):
            row = pl.multiple_of(i * tile, tile)
            rows = pl.ds(pl.multiple_of(first + row, tile), tile)
            cols = arrived[chunk].reshape(expert_count * cap, LANE)
            into[pl.ds(row, tile), :] = jnp.dot(hidden_t[rows, :], cols, preferred_element_type=jnp.float32)
            return carry

        lax.fori_loop(0, half // tile, one, 0)

    def finish(chunk):
        code_copy(chunk).wait_recv()
        scale_copy(chunk).wait_recv()
        step = scale_in[chunk, 0:1, :]
        total[chunk] = own[chunk] + code_in[chunk].astype(jnp.float32) * step
        store(chunk).start()

    def work(chunk, carry):
        all_blocks(chunk).wait_recv()
        local(chunk).wait()
        multiply(chunk, other_start, other)
        part = other[...]
        top = jnp.maximum(jnp.max(jnp.abs(part), axis=0, keepdims=True), 1e-30)
        code[chunk] = jnp.floor(part * (32766.0 / top) + 0.5).astype(jnp.int16)
        scale[chunk] = jnp.broadcast_to(top * (1.0 / 32766.0), scale.shape[1:])
        code_copy(chunk).start()
        scale_copy(chunk).start()
        multiply(chunk, own_start, own.at[chunk])

        @pl.when(chunk > 0)
        def _():
            finish(chunk - 1)

        return carry

    lax.fori_loop(0, chunks, work, 0)
    finish(chunks - 1)

    def drain(chunk, carry):
        all_blocks(chunk).wait_send()
        code_copy(chunk).wait_send()
        scale_copy(chunk).wait_send()
        store(chunk).wait()
        return carry

    lax.fori_loop(0, chunks, drain, 0)


def adamw_kernel(total_ref, master_ref, moment1_ref, moment2_ref, master_out, moment1_out, moment2_out):
    summed = total_ref[...]
    new_moment1 = 0.9 * moment1_ref[0, 0] + 0.1 * summed
    new_moment2 = 0.95 * moment2_ref[0, 0] + 0.05 * summed * summed
    master = master_ref[0, 0]
    update = new_moment1 / (1.0 - 0.9**10) / (jnp.sqrt(new_moment2 / (1.0 - 0.95**10)) + 1e-08)
    master_out[0, 0] = master - 0.2 * (update + 0.05 * master)
    moment1_out[0, 0] = new_moment1
    moment2_out[0, 0] = new_moment2


def body(out_grad, routes, saved_hidden, master, moment1, moment2):
    expert_count = lax.axis_size("expert")
    slots, width = out_grad.shape
    cap, hid = saved_hidden.shape[3:]
    half, cols = master.shape[2:]
    chunks = cols // LANE
    bf16, f32 = jnp.bfloat16, jnp.float32
    dma = pltpu.SemaphoreType.DMA
    total = pl.pallas_call(
        exchange_kernel,
        out_shape=jax.ShapeDtypeStruct((half, cols), f32),
        in_specs=[
            pl.BlockSpec(memory_space=pl.ANY),
            pl.BlockSpec(memory_space=pltpu.VMEM),
            pl.BlockSpec(memory_space=pl.ANY),
        ],
        out_specs=pl.BlockSpec(memory_space=pl.ANY),
        scratch_shapes=[
            pltpu.VMEM((slots, width), bf16),
            pltpu.VMEM((EXPG * cap, slots), bf16),
            pltpu.VMEM((chunks, expert_count, cap, LANE), bf16),
            pltpu.VMEM((chunks, expert_count, cap, LANE), bf16),
            pltpu.VMEM((expert_count, cap, hid), bf16),
            pltpu.VMEM((hid, expert_count * cap), bf16),
            pltpu.VMEM((chunks, half, LANE), f32),
            pltpu.VMEM((half, LANE), f32),
            pltpu.VMEM((chunks, half, LANE), jnp.int16),
            pltpu.VMEM((chunks, half, LANE), jnp.int16),
            pltpu.VMEM((chunks, 8, LANE), f32),
            pltpu.VMEM((chunks, 8, LANE), f32),
            pltpu.VMEM((chunks, half, LANE), f32),
            dma((2,)),
        ] + [dma((chunks,))] * 8,
        compiler_params=pltpu.CompilerParams(
            collective_id=0, has_side_effects=True, vmem_limit_bytes=56 * 1024 * 1024
        ),
        cost_estimate=pl.CostEstimate(
            flops=2 * expert_count * cap * hid * cols, bytes_accessed=16 << 20, transcendentals=0
        ),
        name="exchange",
    )(out_grad, routes.reshape(1, slots), saved_hidden)
    rows = 64
    state = pl.BlockSpec((1, 1, rows, cols), lambda i: (0, 0, i, 0))
    shape = jax.ShapeDtypeStruct((1, 1, half, cols), f32)
    return pl.pallas_call(
        adamw_kernel,
        grid=(half // rows,),
        out_shape=(shape, shape, shape),
        in_specs=[pl.BlockSpec((rows, cols), lambda i: (i, 0)), state, state, state],
        out_specs=(state, state, state),
        name="adamw",
    )(total, master, moment1, moment2)


def solution(mesh):
    in_specs = (
        P(("pipe", "expert"), None),
        P(("pipe", "expert"), None),
        P("pipe", "expert", None, None, None),
        P("pipe", "expert", None, None),
        P("pipe", "expert", None, None),
        P("pipe", "expert", None, None),
    )
    out_specs = (
        P("pipe", "expert", None, None),
        P("pipe", "expert", None, None),
        P("pipe", "expert", None, None),
    )
    return jax.shard_map(body, mesh=mesh, in_specs=in_specs, out_specs=out_specs, check_vma=False)
```

```python
import jax
import jax.numpy as jnp
from jax import lax
from jax.experimental import pallas as pl
from jax.experimental.pallas import tpu as pltpu
from jax.sharding import PartitionSpec as P

EXPG = 4
LANE = 128
LAG = 3
MESH = pl.DeviceIdType.MESH


def exchange_kernel(
    grad_hbm, routes_ref, hidden_hbm, master_hbm, moment1_hbm, moment2_hbm, master, moment1, moment2,
    grad, place, outbound, arrived, hidden, hidden_t, own, other, code, code_in, scale, scale_in,
    load_sem, local_sem, send_sem, recv_sem, code_send, code_recv, scale_send, scale_recv,
):
    pipe, me = lax.axis_index("pipe"), lax.axis_index("expert")
    pipe_count, expert_count = lax.axis_size("pipe"), lax.axis_size("expert")
    chunks, _, cap, _ = outbound.shape
    slots, width = grad.shape
    split = expert_count // EXPG
    slab = width // split
    hid = hidden_t.shape[0]
    half = hid // 2
    mirror = pipe_count - 1 - pipe
    keep_high = pipe // (pipe_count // 2)
    own_start = pl.multiple_of(keep_high * half, half)
    other_start = pl.multiple_of((1 - keep_high) * half, half)
    tile = half // 2

    load_grad = pltpu.make_async_copy(grad_hbm, grad, load_sem.at[0])
    load_grad.start()
    load_hidden = pltpu.make_async_copy(hidden_hbm.at[0, 0], hidden, load_sem.at[1])
    load_hidden.start()
    load_state = [
        pltpu.make_async_copy(src.at[0, 0], dst, load_sem.at[2 + i])
        for i, (src, dst) in enumerate(((master_hbm, master), (moment1_hbm, moment1), (moment2_hbm, moment2)))
    ]
    for load in load_state:
        load.start()

    barrier = pltpu.get_barrier_semaphore()

    def greet(step, carry):
        pl.semaphore_signal(
            barrier, inc=1, device_id=(pipe, lax.rem(me + step, expert_count)), device_id_type=MESH
        )
        return carry

    lax.fori_loop(1, expert_count, greet, 0)
    pl.semaphore_signal(barrier, inc=1, device_id=(mirror, me), device_id_type=MESH)

    route = routes_ref[...]
    chosen = jnp.broadcast_to(route, (8, slots)) == lax.broadcasted_iota(jnp.int32, (8, slots), 0)
    earlier = lax.broadcasted_iota(jnp.int32, (slots, slots), 0) < lax.broadcasted_iota(jnp.int32, (slots, slots), 1)
    before = jnp.dot(
        chosen.astype(jnp.bfloat16), earlier.astype(jnp.bfloat16), preferred_element_type=jnp.float32
    )
    rank = jnp.sum(jnp.where(chosen, before, 0.0), axis=0, keepdims=True).astype(jnp.int32)
    flat = jnp.broadcast_to(route * cap + rank, (EXPG * cap, slots))
    placed = flat == lax.broadcasted_iota(jnp.int32, (EXPG * cap, slots), 0)
    place[...] = placed.astype(jnp.bfloat16)

    load_grad.wait()

    def block(chunk, peer):
        return pltpu.make_async_remote_copy(
            src_ref=outbound.at[chunk, peer],
            dst_ref=arrived.at[chunk, me],
            send_sem=send_sem.at[chunk],
            recv_sem=recv_sem.at[chunk],
            device_id=(pipe, peer),
            device_id_type=MESH,
        )

    def local(chunk):
        return pltpu.make_async_copy(outbound.at[chunk, me], arrived.at[chunk, me], local_sem.at[chunk])

    def pick_send(chunk, carry):
        for step in range(split):
            j = lax.rem(me + step, split)
            start = pl.multiple_of(j * slab + chunk * LANE, LANE)
            picked = jnp.dot(place[...], grad[:, pl.ds(start, LANE)], preferred_element_type=jnp.float32)
            picked = picked.astype(jnp.bfloat16)
            for k in range(EXPG):
                outbound[chunk, k * split + j] = picked[k * cap:(k + 1) * cap]
            for turn_k in range(EXPG):
                k = lax.rem(me // split + EXPG - 1 - turn_k, EXPG)
                if step == 0 and turn_k == EXPG - 1:
                    local(chunk).start()
                else:
                    block(chunk, k * split + j).start()
        return carry

    def all_blocks(chunk):
        others = pl.ds(0, expert_count - 1)
        return pltpu.make_async_remote_copy(
            src_ref=outbound.at[chunk, others],
            dst_ref=arrived.at[chunk, others],
            send_sem=send_sem.at[chunk],
            recv_sem=recv_sem.at[chunk],
            device_id=(pipe, me),
            device_id_type=MESH,
        )

    pl.semaphore_wait(barrier, expert_count)
    lax.fori_loop(0, chunks, pick_send, 0)

    load_hidden.wait()

    def turn(s, carry):
        at = pl.multiple_of(s * cap, cap)
        hidden_t[:, pl.ds(at, cap)] = hidden[s].T
        return carry

    lax.fori_loop(0, expert_count, turn, 0)

    def code_copy(chunk):
        return pltpu.make_async_remote_copy(
            src_ref=code.at[chunk], dst_ref=code_in.at[chunk],
            send_sem=code_send.at[chunk], recv_sem=code_recv.at[chunk],
            device_id=(mirror, me), device_id_type=MESH,
        )

    def scale_copy(chunk):
        return pltpu.make_async_remote_copy(
            src_ref=scale.at[chunk], dst_ref=scale_in.at[chunk],
            send_sem=scale_send.at[chunk], recv_sem=scale_recv.at[chunk],
            device_id=(mirror, me), device_id_type=MESH,
        )

    def multiply(chunk, first, into):
        def one(i, carry):
            row = pl.multiple_of(i * tile, tile)
            rows = pl.ds(pl.multiple_of(first + row, tile), tile)
            cols = arrived[chunk].reshape(expert_count * cap, LANE)
            into[pl.ds(row, tile), :] = jnp.dot(hidden_t[rows, :], cols, preferred_element_type=jnp.float32)
            return carry

        lax.fori_loop(0, half // tile, one, 0)

    def finish(chunk):
        code_copy(chunk).wait_recv()
        scale_copy(chunk).wait_recv()
        summed = own[chunk] + code_in[chunk].astype(jnp.float32) * scale_in[chunk, 0:1, :]
        cols = pl.ds(pl.multiple_of(chunk * LANE, LANE), LANE)
        new_moment1 = 0.9 * moment1[:, cols] + 0.1 * summed
        new_moment2 = 0.95 * moment2[:, cols] + 0.05 * summed * summed
        weight = master[:, cols]
        update = new_moment1 / (1.0 - 0.9**10) / (jnp.sqrt(new_moment2 / (1.0 - 0.95**10)) + 1e-08)
        master[:, cols] = weight - 0.2 * (update + 0.05 * weight)
        moment1[:, cols] = new_moment1
        moment2[:, cols] = new_moment2

    def work(chunk, carry):
        all_blocks(chunk).wait_recv()
        local(chunk).wait()
        multiply(chunk, other_start, other)
        part = other[...]
        top = jnp.maximum(jnp.max(jnp.abs(part), axis=0, keepdims=True), 1e-30)
        code[chunk] = jnp.floor(part * (32766.0 / top) + 0.5).astype(jnp.int16)
        scale[chunk] = jnp.broadcast_to(top * (1.0 / 32766.0), scale.shape[1:])
        code_copy(chunk).start()
        scale_copy(chunk).start()
        multiply(chunk, own_start, own.at[chunk])

        @pl.when(chunk >= LAG)
        def _():
            finish(chunk - LAG)

        return carry

    for load in load_state:
        load.wait()
    lax.fori_loop(0, chunks, work, 0)

    def finish_rest(chunk, carry):
        finish(chunk)
        return carry

    lax.fori_loop(chunks - LAG, chunks, finish_rest, 0)

    def drain(chunk, carry):
        all_blocks(chunk).wait_send()
        code_copy(chunk).wait_send()
        scale_copy(chunk).wait_send()
        return carry

    lax.fori_loop(0, chunks, drain, 0)


def body(out_grad, routes, saved_hidden, master, moment1, moment2):
    expert_count = lax.axis_size("expert")
    slots, width = out_grad.shape
    cap, hid = saved_hidden.shape[3:]
    half, cols = master.shape[2:]
    chunks = cols // LANE
    bf16, f32 = jnp.bfloat16, jnp.float32
    dma = pltpu.SemaphoreType.DMA
    state = pltpu.VMEM((half, cols), f32)
    states = pl.pallas_call(
        exchange_kernel,
        out_shape=(state, state, state),
        in_specs=[
            pl.BlockSpec(memory_space=pl.ANY),
            pl.BlockSpec(memory_space=pltpu.VMEM),
            pl.BlockSpec(memory_space=pl.ANY),
            pl.BlockSpec(memory_space=pl.ANY),
            pl.BlockSpec(memory_space=pl.ANY),
            pl.BlockSpec(memory_space=pl.ANY),
        ],
        out_specs=[pl.BlockSpec(memory_space=pltpu.VMEM)] * 3,
        scratch_shapes=[
            pltpu.VMEM((slots, width), bf16),
            pltpu.VMEM((EXPG * cap, slots), bf16),
            pltpu.VMEM((chunks, expert_count, cap, LANE), bf16),
            pltpu.VMEM((chunks, expert_count, cap, LANE), bf16),
            pltpu.VMEM((expert_count, cap, hid), bf16),
            pltpu.VMEM((hid, expert_count * cap), bf16),
            pltpu.VMEM((chunks, half, LANE), f32),
            pltpu.VMEM((half, LANE), f32),
            pltpu.VMEM((chunks, half, LANE), jnp.int16),
            pltpu.VMEM((chunks, half, LANE), jnp.int16),
            pltpu.VMEM((chunks, 8, LANE), f32),
            pltpu.VMEM((chunks, 8, LANE), f32),
            dma((5,)),
        ] + [dma((chunks,))] * 7,
        compiler_params=pltpu.CompilerParams(
            collective_id=0, has_side_effects=True, vmem_limit_bytes=48 * 1024 * 1024
        ),
        cost_estimate=pl.CostEstimate(
            flops=2 * expert_count * cap * hid * cols, bytes_accessed=16 << 20, transcendentals=0
        ),
        name="exchange",
    )(out_grad, routes.reshape(1, slots), saved_hidden, master, moment1, moment2)
    return tuple(new.reshape(1, 1, half, cols) for new in states)


def solution(mesh):
    in_specs = (
        P(("pipe", "expert"), None),
        P(("pipe", "expert"), None),
        P("pipe", "expert", None, None, None),
        P("pipe", "expert", None, None),
        P("pipe", "expert", None, None),
        P("pipe", "expert", None, None),
    )
    out_specs = (
        P("pipe", "expert", None, None),
        P("pipe", "expert", None, None),
        P("pipe", "expert", None, None),
    )
    return jax.shard_map(body, mesh=mesh, in_specs=in_specs, out_specs=out_specs, check_vma=False)
```

```python
import jax
import jax.numpy as jnp
from jax import lax
from jax.experimental import pallas as pl
from jax.experimental.pallas import tpu as pltpu
from jax.sharding import PartitionSpec as P

EXPG = 4
LANE = 128
LAG = 3
MESH = pl.DeviceIdType.MESH


def exchange_kernel(
    grad_hbm, routes_hbm, hidden_hbm, master_hbm, moment1_hbm, moment2_hbm, master, moment1, moment2,
    grad, routes, place, outbound, arrived, hidden, hidden_t, own, other, code, code_in, scale, scale_in,
    load_sem, local_sem, send_sem, recv_sem, code_send, code_recv, scale_send, scale_recv,
):
    pipe, me = lax.axis_index("pipe"), lax.axis_index("expert")
    pipe_count, expert_count = lax.axis_size("pipe"), lax.axis_size("expert")
    chunks, _, cap, _ = outbound.shape
    slots, width = grad.shape
    split = expert_count // EXPG
    slab = width // split
    hid = hidden_t.shape[0]
    half = hid // 2
    mirror = pipe_count - 1 - pipe
    keep_high = pipe // (pipe_count // 2)
    own_start = pl.multiple_of(keep_high * half, half)
    other_start = pl.multiple_of((1 - keep_high) * half, half)
    tile = half // 2

    load_grad = pltpu.make_async_copy(grad_hbm, grad, load_sem.at[0])
    load_grad.start()
    load_routes = pltpu.make_async_copy(routes_hbm, routes, load_sem.at[5])
    load_routes.start()
    load_hidden = pltpu.make_async_copy(hidden_hbm.at[0, 0], hidden, load_sem.at[1])
    load_hidden.start()
    load_state = [
        pltpu.make_async_copy(src.at[0, 0], dst, load_sem.at[2 + i])
        for i, (src, dst) in enumerate(((master_hbm, master), (moment1_hbm, moment1), (moment2_hbm, moment2)))
    ]
    for load in load_state:
        load.start()

    barrier = pltpu.get_barrier_semaphore()

    def greet(step, carry):
        pl.semaphore_signal(
            barrier, inc=1, device_id=(pipe, lax.rem(me + step, expert_count)), device_id_type=MESH
        )
        return carry

    lax.fori_loop(1, expert_count, greet, 0)
    pl.semaphore_signal(barrier, inc=1, device_id=(mirror, me), device_id_type=MESH)

    load_routes.wait()
    route = routes[...]
    chosen = jnp.broadcast_to(route, (8, slots)) == lax.broadcasted_iota(jnp.int32, (8, slots), 0)
    earlier = lax.broadcasted_iota(jnp.int32, (slots, slots), 0) < lax.broadcasted_iota(jnp.int32, (slots, slots), 1)
    before = jnp.dot(
        chosen.astype(jnp.bfloat16), earlier.astype(jnp.bfloat16), preferred_element_type=jnp.float32
    )
    rank = jnp.sum(jnp.where(chosen, before, 0.0), axis=0, keepdims=True).astype(jnp.int32)
    flat = jnp.broadcast_to(route * cap + rank, (EXPG * cap, slots))
    placed = flat == lax.broadcasted_iota(jnp.int32, (EXPG * cap, slots), 0)
    place[...] = placed.astype(jnp.bfloat16)

    load_grad.wait()

    def block(chunk, peer):
        return pltpu.make_async_remote_copy(
            src_ref=outbound.at[chunk, peer],
            dst_ref=arrived.at[chunk, me],
            send_sem=send_sem.at[chunk],
            recv_sem=recv_sem.at[chunk],
            device_id=(pipe, peer),
            device_id_type=MESH,
        )

    def local(chunk):
        return pltpu.make_async_copy(outbound.at[chunk, me], arrived.at[chunk, me], local_sem.at[chunk])

    def pick_send(chunk, carry):
        for step in range(split):
            j = lax.rem(me + step, split)
            start = pl.multiple_of(j * slab + chunk * LANE, LANE)
            picked = jnp.dot(place[...], grad[:, pl.ds(start, LANE)], preferred_element_type=jnp.float32)
            picked = picked.astype(jnp.bfloat16)
            for k in range(EXPG):
                outbound[chunk, k * split + j] = picked[k * cap:(k + 1) * cap]
            for turn_k in range(EXPG):
                k = lax.rem(me // split + EXPG - 1 - turn_k, EXPG)
                if step == 0 and turn_k == EXPG - 1:
                    local(chunk).start()
                else:
                    block(chunk, k * split + j).start()
        return carry

    def all_blocks(chunk):
        others = pl.ds(0, expert_count - 1)
        return pltpu.make_async_remote_copy(
            src_ref=outbound.at[chunk, others],
            dst_ref=arrived.at[chunk, others],
            send_sem=send_sem.at[chunk],
            recv_sem=recv_sem.at[chunk],
            device_id=(pipe, me),
            device_id_type=MESH,
        )

    pl.semaphore_wait(barrier, expert_count)
    lax.fori_loop(0, chunks, pick_send, 0)

    load_hidden.wait()

    def turn(s, carry):
        at = pl.multiple_of(s * cap, cap)
        hidden_t[:, pl.ds(at, cap)] = hidden[s].T
        return carry

    lax.fori_loop(0, expert_count, turn, 0)

    def code_copy(chunk):
        return pltpu.make_async_remote_copy(
            src_ref=code.at[chunk], dst_ref=code_in.at[chunk],
            send_sem=code_send.at[chunk], recv_sem=code_recv.at[chunk],
            device_id=(mirror, me), device_id_type=MESH,
        )

    def scale_copy(chunk):
        return pltpu.make_async_remote_copy(
            src_ref=scale.at[chunk], dst_ref=scale_in.at[chunk],
            send_sem=scale_send.at[chunk], recv_sem=scale_recv.at[chunk],
            device_id=(mirror, me), device_id_type=MESH,
        )

    def multiply(chunk, first, into):
        def one(i, carry):
            row = pl.multiple_of(i * tile, tile)
            rows = pl.ds(pl.multiple_of(first + row, tile), tile)
            cols = arrived[chunk].reshape(expert_count * cap, LANE)
            into[pl.ds(row, tile), :] = jnp.dot(hidden_t[rows, :], cols, preferred_element_type=jnp.float32)
            return carry

        lax.fori_loop(0, half // tile, one, 0)

    def finish(chunk):
        code_copy(chunk).wait_recv()
        scale_copy(chunk).wait_recv()
        summed = own[chunk] + code_in[chunk].astype(jnp.float32) * scale_in[chunk, 0:1, :]
        cols = pl.ds(pl.multiple_of(chunk * LANE, LANE), LANE)
        new_moment1 = 0.9 * moment1[:, cols] + 0.1 * summed
        new_moment2 = 0.95 * moment2[:, cols] + 0.05 * summed * summed
        weight = master[:, cols]
        update = new_moment1 / (1.0 - 0.9**10) / (jnp.sqrt(new_moment2 / (1.0 - 0.95**10)) + 1e-08)
        master[:, cols] = weight - 0.2 * (update + 0.05 * weight)
        moment1[:, cols] = new_moment1
        moment2[:, cols] = new_moment2

    def work(chunk, carry):
        all_blocks(chunk).wait_recv()
        local(chunk).wait()
        multiply(chunk, other_start, other)
        part = other[...]
        top = jnp.maximum(jnp.max(jnp.abs(part), axis=0, keepdims=True), 1e-30)
        code[chunk] = jnp.floor(part * (32766.0 / top) + 0.5).astype(jnp.int16)
        scale[chunk] = jnp.broadcast_to(top * (1.0 / 32766.0), scale.shape[1:])
        code_copy(chunk).start()
        scale_copy(chunk).start()
        multiply(chunk, own_start, own.at[chunk])

        @pl.when(chunk >= LAG)
        def _():
            finish(chunk - LAG)

        return carry

    for load in load_state:
        load.wait()
    lax.fori_loop(0, chunks, work, 0)

    def finish_rest(chunk, carry):
        finish(chunk)
        return carry

    lax.fori_loop(chunks - LAG, chunks, finish_rest, 0)

    def drain(chunk, carry):
        all_blocks(chunk).wait_send()
        code_copy(chunk).wait_send()
        scale_copy(chunk).wait_send()
        return carry

    lax.fori_loop(0, chunks, drain, 0)


def store_kernel(*refs):
    count = len(refs) // 2
    sems = refs[-1]
    copies = [
        pltpu.make_async_copy(refs[i], refs[count + i].at[0, 0], sems.at[i]) for i in range(count)
    ]
    for copy in copies:
        copy.start()
    for copy in copies:
        copy.wait()


def body(out_grad, routes, saved_hidden, master, moment1, moment2):
    expert_count = lax.axis_size("expert")
    slots, width = out_grad.shape
    cap, hid = saved_hidden.shape[3:]
    half, cols = master.shape[2:]
    chunks = cols // LANE
    bf16, f32 = jnp.bfloat16, jnp.float32
    dma = pltpu.SemaphoreType.DMA
    state = pltpu.VMEM((half, cols), f32)
    states = pl.pallas_call(
        exchange_kernel,
        out_shape=(state, state, state),
        in_specs=[
            pl.BlockSpec(memory_space=pl.ANY),
            pl.BlockSpec(memory_space=pltpu.HBM),
            pl.BlockSpec(memory_space=pl.ANY),
            pl.BlockSpec(memory_space=pl.ANY),
            pl.BlockSpec(memory_space=pl.ANY),
            pl.BlockSpec(memory_space=pl.ANY),
        ],
        out_specs=[pl.BlockSpec(memory_space=pltpu.VMEM)] * 3,
        scratch_shapes=[
            pltpu.VMEM((slots, width), bf16),
            pltpu.VMEM((1, slots), jnp.int32),
            pltpu.VMEM((EXPG * cap, slots), bf16),
            pltpu.VMEM((chunks, expert_count, cap, LANE), bf16),
            pltpu.VMEM((chunks, expert_count, cap, LANE), bf16),
            pltpu.VMEM((expert_count, cap, hid), bf16),
            pltpu.VMEM((hid, expert_count * cap), bf16),
            pltpu.VMEM((chunks, half, LANE), f32),
            pltpu.VMEM((half, LANE), f32),
            pltpu.VMEM((chunks, half, LANE), jnp.int16),
            pltpu.VMEM((chunks, half, LANE), jnp.int16),
            pltpu.VMEM((chunks, 8, LANE), f32),
            pltpu.VMEM((chunks, 8, LANE), f32),
            dma((6,)),
        ] + [dma((chunks,))] * 7,
        compiler_params=pltpu.CompilerParams(
            collective_id=0, has_side_effects=True, vmem_limit_bytes=48 * 1024 * 1024
        ),
        cost_estimate=pl.CostEstimate(
            flops=2 * expert_count * cap * hid * cols, bytes_accessed=16 << 20, transcendentals=0
        ),
        name="exchange",
    )(out_grad, pltpu.with_memory_space_constraint(routes.reshape(1, slots), pltpu.HBM), saved_hidden, master, moment1, moment2)
    shape = jax.ShapeDtypeStruct((1, 1, half, cols), f32)
    return pl.pallas_call(
        store_kernel,
        out_shape=(shape, shape, shape),
        in_specs=[pl.BlockSpec(memory_space=pltpu.VMEM)] * 3,
        out_specs=[pl.BlockSpec(memory_space=pl.ANY)] * 3,
        scratch_shapes=[dma((3,))],
        compiler_params=pltpu.CompilerParams(vmem_limit_bytes=1024 * 1024),
        name="store",
    )(*(pltpu.with_memory_space_constraint(new, pltpu.VMEM) for new in states))


def solution(mesh):
    in_specs = (
        P(("pipe", "expert"), None),
        P(("pipe", "expert"), None),
        P("pipe", "expert", None, None, None),
        P("pipe", "expert", None, None),
        P("pipe", "expert", None, None),
        P("pipe", "expert", None, None),
    )
    out_specs = (
        P("pipe", "expert", None, None),
        P("pipe", "expert", None, None),
        P("pipe", "expert", None, None),
    )
    return jax.shard_map(body, mesh=mesh, in_specs=in_specs, out_specs=out_specs, check_vma=False)
```

```python
import jax
import jax.numpy as jnp
from jax import lax
from jax.experimental import pallas as pl
from jax.experimental.pallas import tpu as pltpu
from jax.sharding import PartitionSpec as P

EXPG = 4
LANE = 128
LAG = 3
AHEAD = 3
CROSSING = 208
MESH = pl.DeviceIdType.MESH


def exchange_kernel(
    grad_hbm, routes_hbm, hidden_hbm, master_hbm, moment1_hbm, moment2_hbm, master, moment1, moment2,
    grad, routes, place, outbound, arrived, hidden, hidden_t, own, other, code, code_in, scale, scale_in,
    load_sem, local_sem, send_sem, recv_sem, code_send, code_recv, scale_send, scale_recv,
):
    pipe, me = lax.axis_index("pipe"), lax.axis_index("expert")
    pipe_count, expert_count = lax.axis_size("pipe"), lax.axis_size("expert")
    chunks, _, cap, _ = outbound.shape
    slots, width = grad.shape
    split = expert_count // EXPG
    slab = width // split
    hid = hidden_t.shape[0]
    half = hid // 2
    mirror = pipe_count - 1 - pipe
    keep_high = pipe // (pipe_count // 2)
    own_start = pl.multiple_of(keep_high * half, half)
    other_start = pl.multiple_of((1 - keep_high) * half, half)
    tile = half // 2

    load_grad = pltpu.make_async_copy(grad_hbm, grad, load_sem.at[0])
    load_grad.start()
    load_routes = pltpu.make_async_copy(routes_hbm, routes, load_sem.at[5])
    load_routes.start()
    load_hidden = pltpu.make_async_copy(hidden_hbm.at[0, 0], hidden, load_sem.at[1])
    load_hidden.start()
    load_state = [
        pltpu.make_async_copy(src.at[0, 0], dst, load_sem.at[2 + i])
        for i, (src, dst) in enumerate(((master_hbm, master), (moment1_hbm, moment1), (moment2_hbm, moment2)))
    ]
    for load in load_state:
        load.start()

    barrier = pltpu.get_barrier_semaphore()

    def greet(step, carry):
        pl.semaphore_signal(
            barrier, inc=1, device_id=(pipe, lax.rem(me + step, expert_count)), device_id_type=MESH
        )
        return carry

    lax.fori_loop(1, expert_count, greet, 0)
    pl.semaphore_signal(barrier, inc=1, device_id=(mirror, me), device_id_type=MESH)

    load_routes.wait()
    route = routes[...]
    chosen = jnp.broadcast_to(route, (8, slots)) == lax.broadcasted_iota(jnp.int32, (8, slots), 0)
    earlier = lax.broadcasted_iota(jnp.int32, (slots, slots), 0) < lax.broadcasted_iota(jnp.int32, (slots, slots), 1)
    before = jnp.dot(
        chosen.astype(jnp.bfloat16), earlier.astype(jnp.bfloat16), preferred_element_type=jnp.float32
    )
    rank = jnp.sum(jnp.where(chosen, before, 0.0), axis=0, keepdims=True).astype(jnp.int32)
    flat = jnp.broadcast_to(route * cap + rank, (EXPG * cap, slots))
    placed = flat == lax.broadcasted_iota(jnp.int32, (EXPG * cap, slots), 0)
    place[...] = placed.astype(jnp.bfloat16)

    load_grad.wait()

    def block(chunk, peer):
        return pltpu.make_async_remote_copy(
            src_ref=outbound.at[chunk, peer],
            dst_ref=arrived.at[chunk, me],
            send_sem=send_sem.at[chunk],
            recv_sem=recv_sem.at[chunk],
            device_id=(pipe, peer),
            device_id_type=MESH,
        )

    def local(chunk):
        return pltpu.make_async_copy(outbound.at[chunk, me], arrived.at[chunk, me], local_sem.at[chunk])

    def pick_send(chunk, carry):
        for step in range(split):
            j = lax.rem(me + step, split)
            start = pl.multiple_of(j * slab + chunk * LANE, LANE)
            picked = jnp.dot(place[...], grad[:, pl.ds(start, LANE)], preferred_element_type=jnp.float32)
            picked = picked.astype(jnp.bfloat16)
            for k in range(EXPG):
                outbound[chunk, k * split + j] = picked[k * cap:(k + 1) * cap]
            for turn_k in range(EXPG):
                k = lax.rem(me // split + EXPG - 1 - turn_k, EXPG)
                if step == 0 and turn_k == EXPG - 1:
                    local(chunk).start()
                else:
                    block(chunk, k * split + j).start()
        return carry

    def all_blocks(chunk):
        others = pl.ds(0, expert_count - 1)
        return pltpu.make_async_remote_copy(
            src_ref=outbound.at[chunk, others],
            dst_ref=arrived.at[chunk, others],
            send_sem=send_sem.at[chunk],
            recv_sem=recv_sem.at[chunk],
            device_id=(pipe, me),
            device_id_type=MESH,
        )

    pl.semaphore_wait(barrier, expert_count)
    lax.fori_loop(0, chunks, pick_send, 0)

    load_hidden.wait()

    def turn(s, carry):
        at = pl.multiple_of(s * cap, cap)
        hidden_t[:, pl.ds(at, cap)] = hidden[s].T
        return carry

    lax.fori_loop(0, expert_count, turn, 0)

    def code_copy(chunk):
        return pltpu.make_async_remote_copy(
            src_ref=code.at[chunk], dst_ref=code_in.at[chunk],
            send_sem=code_send.at[chunk], recv_sem=code_recv.at[chunk],
            device_id=(mirror, me), device_id_type=MESH,
        )

    def scale_copy(chunk):
        return pltpu.make_async_remote_copy(
            src_ref=scale.at[chunk], dst_ref=scale_in.at[chunk],
            send_sem=scale_send.at[chunk], recv_sem=scale_recv.at[chunk],
            device_id=(mirror, me), device_id_type=MESH,
        )

    def multiply(chunk, first, into):
        def one(i, carry):
            row = pl.multiple_of(i * tile, tile)
            rows = pl.ds(pl.multiple_of(first + row, tile), tile)
            cols = arrived[chunk].reshape(expert_count * cap, LANE)
            into[pl.ds(row, tile), :] = jnp.dot(hidden_t[rows, :], cols, preferred_element_type=jnp.float32)
            return carry

        lax.fori_loop(0, half // tile, one, 0)

    def finish(chunk):
        code_copy(chunk).wait_recv()
        scale_copy(chunk).wait_recv()
        summed = own[chunk] + code_in[chunk].astype(jnp.float32) * scale_in[chunk, 0:1, :]
        cols = pl.ds(pl.multiple_of(chunk * LANE, LANE), LANE)
        new_moment1 = 0.9 * moment1[:, cols] + 0.1 * summed
        new_moment2 = 0.95 * moment2[:, cols] + 0.05 * summed * summed
        weight = master[:, cols]
        update = new_moment1 / (1.0 - 0.9**10) / (jnp.sqrt(new_moment2 / (1.0 - 0.95**10)) + 1e-08)
        master[:, cols] = weight - 0.2 * (update + 0.05 * weight)
        moment1[:, cols] = new_moment1
        moment2[:, cols] = new_moment2

    def work(chunk, carry):
        all_blocks(chunk).wait_recv()
        local(chunk).wait()
        multiply(chunk, other_start, other)
        part = other[...]
        top = jnp.maximum(jnp.max(jnp.abs(part), axis=0, keepdims=True), 1e-30)
        code[chunk] = jnp.floor(part * (32766.0 / top) + 0.5).astype(jnp.int16)
        scale[chunk] = jnp.broadcast_to(top * (1.0 / 32766.0), scale.shape[1:])
        code_copy(chunk).start()
        scale_copy(chunk).start()
        multiply(chunk, own_start, own.at[chunk])

        @pl.when(chunk >= LAG)
        def _():
            finish(chunk - LAG)

        return carry

    for load in load_state:
        load.wait()
    lax.fori_loop(0, chunks, work, 0)

    def finish_rest(chunk, carry):
        finish(chunk)
        return carry

    lax.fori_loop(chunks - LAG, chunks, finish_rest, 0)

    def drain(chunk, carry):
        all_blocks(chunk).wait_send()
        code_copy(chunk).wait_send()
        scale_copy(chunk).wait_send()
        return carry

    lax.fori_loop(0, chunks, drain, 0)


def relay_kernel(
    grad_hbm, routes_hbm, hidden_hbm, master_hbm, moment1_hbm, moment2_hbm, master, moment1, moment2, over_out,
    grad, routes, routes_in, place, pack, expand, packed, packed_in, outbound, arrived, hidden, hidden_t,
    own, other, code, code_in, scale, scale_in, over_plane, over_pair, over_pipe,
    load_sem, hidden_sem, routes_sem, over_sem, pack_send, pack_recv, local_sem, send_sem, recv_sem,
    code_send, code_recv, scale_send, scale_recv,
):
    pipe, me = lax.axis_index("pipe"), lax.axis_index("expert")
    pipe_count, expert_count = lax.axis_size("pipe"), lax.axis_size("expert")
    chunks, _, plane, cap, _ = outbound.shape
    slots, width = grad.shape
    split = expert_count // EXPG
    slab = width // split
    hid = hidden_t.shape[0]
    half = hid // 2
    mirror = pipe_count - 1 - pipe
    keep_high = pipe // (pipe_count // 2)
    own_start = pl.multiple_of(keep_high * half, half)
    other_start = pl.multiple_of((1 - keep_high) * half, half)
    tile = half // 2
    side = me // plane
    seat = me % plane
    base = side * plane
    partner = lax.rem(me + plane, expert_count)
    local_experts = EXPG // 2
    bound = packed.shape[2]

    load_routes = pltpu.make_async_copy(routes_hbm, routes, load_sem.at[0])
    load_routes.start()
    load_grad = pltpu.make_async_copy(grad_hbm, grad, load_sem.at[1])
    load_grad.start()
    group = hidden.shape[1]

    def load_hidden(turn):
        return pltpu.make_async_copy(
            hidden_hbm.at[0, 0, pl.ds(turn * group, group)], hidden.at[turn % 2], hidden_sem.at[turn % 2]
        )

    load_hidden(0).start()
    load_hidden(1).start()
    load_state = [
        pltpu.make_async_copy(src.at[0, 0], dst, load_sem.at[2 + i])
        for i, (src, dst) in enumerate(((master_hbm, master), (moment1_hbm, moment1), (moment2_hbm, moment2)))
    ]
    for load in load_state:
        load.start()

    barrier = pltpu.get_barrier_semaphore()

    def greet(step, carry):
        pl.semaphore_signal(
            barrier, inc=1, device_id=(pipe, base + lax.rem(seat + step, plane)), device_id_type=MESH
        )
        return carry

    lax.fori_loop(1, plane, greet, 0)
    pl.semaphore_signal(barrier, inc=1, device_id=(pipe, partner), device_id_type=MESH)
    for step in range(1, pipe_count):
        pl.semaphore_signal(barrier, inc=1, device_id=(lax.rem(pipe + step, pipe_count), me), device_id_type=MESH)

    def one_hots(route, packed_side):
        expert = lax.broadcasted_iota(jnp.int32, (8, slots), 0)
        chosen = jnp.broadcast_to(route, (8, slots)) == expert
        earlier = lax.broadcasted_iota(jnp.int32, (slots, slots), 0) < lax.broadcasted_iota(jnp.int32, (slots, slots), 1)
        before = jnp.dot(
            chosen.astype(jnp.bfloat16), earlier.astype(jnp.bfloat16), preferred_element_type=jnp.float32
        )
        rank = jnp.sum(jnp.where(chosen, before, 0.0), axis=0, keepdims=True).astype(jnp.int32)
        flat = jnp.broadcast_to((route - side * local_experts) * cap + rank, (local_experts * cap, slots))
        places = flat == lax.broadcasted_iota(jnp.int32, (local_experts * cap, slots), 0)
        first = packed_side * local_experts
        in_side = (expert >= first) & (expert < first + local_experts)
        order = jnp.sum(jnp.where(in_side, before, 0.0), axis=0, keepdims=True).astype(jnp.int32)
        goes = (route >= first) & (route < first + local_experts)
        order = jnp.broadcast_to(jnp.where(goes, order, -1), (bound, slots))
        ranks = order == lax.broadcasted_iota(jnp.int32, (bound, slots), 0)
        return places.astype(jnp.bfloat16), ranks.astype(jnp.bfloat16), goes

    load_routes.wait()
    own_places, own_ranks, goes = one_hots(routes[...], 1 - side)
    place[...] = own_places
    pack[...] = own_ranks
    crossing = jnp.sum(goes.astype(jnp.float32), axis=1, keepdims=True)
    over = jnp.broadcast_to((crossing > bound).astype(jnp.int32), over_pair.shape[1:])
    over_plane[seat] = over

    load_grad.wait()
    pl.semaphore_wait(barrier, plane - 1 + 1 + pipe_count - 1)

    send_routes = pltpu.make_async_remote_copy(
        src_ref=routes, dst_ref=routes_in, send_sem=routes_sem.at[0], recv_sem=routes_sem.at[1],
        device_id=(pipe, partner), device_id_type=MESH,
    )
    send_routes.start()

    def over_to_plane(seat_to):
        return pltpu.make_async_remote_copy(
            src_ref=over_plane.at[seat], dst_ref=over_plane.at[seat],
            send_sem=over_sem.at[0], recv_sem=over_sem.at[1],
            device_id=(pipe, base + seat_to), device_id_type=MESH,
        )

    def tell_plane(step, carry):
        over_to_plane(lax.rem(seat + step, plane)).start()
        return carry

    over_all_plane = pltpu.make_async_remote_copy(
        src_ref=over_plane.at[pl.ds(0, plane - 1)], dst_ref=over_plane.at[pl.ds(0, plane - 1)],
        send_sem=over_sem.at[0], recv_sem=over_sem.at[1],
        device_id=(pipe, partner), device_id_type=MESH,
    )
    over_to_partner = pltpu.make_async_remote_copy(
        src_ref=over_pair.at[0], dst_ref=over_pair.at[1],
        send_sem=over_sem.at[2], recv_sem=over_sem.at[3],
        device_id=(pipe, partner), device_id_type=MESH,
    )
    over_to_pipes = [
        pltpu.make_async_remote_copy(
            src_ref=over_pipe.at[pipe], dst_ref=over_pipe.at[pipe],
            send_sem=over_sem.at[4], recv_sem=over_sem.at[5],
            device_id=(lax.rem(pipe + step, pipe_count), me), device_id_type=MESH,
        )
        for step in range(1, pipe_count)
    ]
    over_all_pipes = pltpu.make_async_remote_copy(
        src_ref=over_pipe.at[pl.ds(0, pipe_count - 1)], dst_ref=over_pipe.at[pl.ds(0, pipe_count - 1)],
        send_sem=over_sem.at[4], recv_sem=over_sem.at[5],
        device_id=(mirror, me), device_id_type=MESH,
    )

    def block(chunk, kind, to):
        return pltpu.make_async_remote_copy(
            src_ref=outbound.at[chunk, kind, to],
            dst_ref=arrived.at[chunk, me if kind == 0 else partner],
            send_sem=send_sem.at[kind, chunk],
            recv_sem=recv_sem.at[kind, chunk],
            device_id=(pipe, base + to),
            device_id_type=MESH,
        )

    def local(chunk, kind):
        return pltpu.make_async_copy(
            outbound.at[chunk, kind, seat],
            arrived.at[chunk, me if kind == 0 else partner],
            local_sem.at[kind, chunk],
        )

    def all_blocks(chunk, kind):
        others = pl.ds(0, plane - 1)
        return pltpu.make_async_remote_copy(
            src_ref=outbound.at[chunk, kind, others],
            dst_ref=arrived.at[chunk, others],
            send_sem=send_sem.at[kind, chunk],
            recv_sem=recv_sem.at[kind, chunk],
            device_id=(pipe, partner),
            device_id_type=MESH,
        )

    def spread(chunk, kind, step, j, rows):
        rows = rows.astype(jnp.bfloat16)
        for k in range(local_experts):
            outbound[chunk, kind, k * split + j] = rows[k * cap:(k + 1) * cap]
        for turn in range(local_experts):
            k = lax.rem(seat // split + local_experts - 1 - turn, local_experts)
            if step == 0 and turn == local_experts - 1:
                local(chunk, kind).start()
            else:
                block(chunk, kind, k * split + j).start()

    def slab_cols(chunk, j):
        return pl.ds(pl.multiple_of(j * slab + chunk * LANE, LANE), LANE)

    def send_own(chunk):
        for step in range(split):
            j = lax.rem(seat + step, split)
            rows = jnp.dot(place[...], grad[:, slab_cols(chunk, j)], preferred_element_type=jnp.float32)
            spread(chunk, 0, step, j, rows)

    def packed_copy(chunk):
        return pltpu.make_async_remote_copy(
            src_ref=packed.at[chunk], dst_ref=packed_in.at[chunk],
            send_sem=pack_send.at[chunk], recv_sem=pack_recv.at[chunk],
            device_id=(pipe, partner), device_id_type=MESH,
        )

    def send_packed(chunk):
        for j in range(split):
            rows = jnp.dot(pack[...], grad[:, slab_cols(chunk, j)], preferred_element_type=jnp.float32)
            packed[chunk, j] = rows.astype(jnp.bfloat16)
        packed_copy(chunk).start()

    def first_sends(chunk, carry):
        send_own(chunk)
        send_packed(chunk)
        return carry

    first_sends(0, 0)
    lax.fori_loop(1, plane, tell_plane, 0)
    lax.fori_loop(1, chunks, first_sends, 0)

    send_routes.wait_recv()
    their_places, their_ranks, _ = one_hots(routes_in[...], side)
    expand[...] = lax.dot_general(
        their_places, their_ranks, (((1,), (1,)), ((), ())), preferred_element_type=jnp.float32
    ).astype(jnp.bfloat16)

    def relay(chunk):
        packed_copy(chunk).wait_recv()
        for step in range(split):
            j = lax.rem(seat + step, split)
            rows = jnp.dot(expand[...], packed_in[chunk, j], preferred_element_type=jnp.float32)
            spread(chunk, 1, step, j, rows)

    relay(0)

    turns = expert_count // group
    for turn in range(turns):
        load_hidden(turn).wait()

        def flip(i, carry):
            at = pl.multiple_of((turn * group + i) * cap, cap)
            hidden_t[:, pl.ds(at, cap)] = hidden[turn % 2, i].T
            return carry

        lax.fori_loop(0, group, flip, 0)
        if turn + 2 < turns:
            load_hidden(turn + 2).start()

    over_all_plane.wait_recv()
    over_pair[0] = jnp.max(over_plane[...], axis=0)
    over_to_partner.start()

    def relay_one(chunk, carry):
        relay(chunk)
        return carry

    lax.fori_loop(1, AHEAD, relay_one, 0)

    over_to_partner.wait_recv()
    over_pipe[pipe] = jnp.maximum(over_pair[0], over_pair[1])
    for copy in over_to_pipes:
        copy.start()

    def code_copy(chunk):
        return pltpu.make_async_remote_copy(
            src_ref=code.at[chunk], dst_ref=code_in.at[chunk],
            send_sem=code_send.at[chunk], recv_sem=code_recv.at[chunk],
            device_id=(mirror, me), device_id_type=MESH,
        )

    def scale_copy(chunk):
        return pltpu.make_async_remote_copy(
            src_ref=scale.at[chunk], dst_ref=scale_in.at[chunk],
            send_sem=scale_send.at[chunk], recv_sem=scale_recv.at[chunk],
            device_id=(mirror, me), device_id_type=MESH,
        )

    def multiply(chunk, first, into):
        def one(i, carry):
            row = pl.multiple_of(i * tile, tile)
            rows = pl.ds(pl.multiple_of(first + row, tile), tile)
            cols = arrived[chunk].reshape(expert_count * cap, LANE)
            into[pl.ds(row, tile), :] = jnp.dot(hidden_t[rows, :], cols, preferred_element_type=jnp.float32)
            return carry

        lax.fori_loop(0, half // tile, one, 0)

    def finish(chunk):
        code_copy(chunk).wait_recv()
        scale_copy(chunk).wait_recv()
        summed = own[chunk] + code_in[chunk].astype(jnp.float32) * scale_in[chunk, 0:1, :]
        cols = pl.ds(pl.multiple_of(chunk * LANE, LANE), LANE)
        new_moment1 = 0.9 * moment1[:, cols] + 0.1 * summed
        new_moment2 = 0.95 * moment2[:, cols] + 0.05 * summed * summed
        weight = master[:, cols]
        update = new_moment1 / (1.0 - 0.9**10) / (jnp.sqrt(new_moment2 / (1.0 - 0.95**10)) + 1e-08)
        master[:, cols] = weight - 0.2 * (update + 0.05 * weight)
        moment1[:, cols] = new_moment1
        moment2[:, cols] = new_moment2

    def work(chunk, carry):
        @pl.when(chunk + AHEAD < chunks)
        def _():
            relay(chunk + AHEAD)

        for kind in range(2):
            all_blocks(chunk, kind).wait_recv()
            local(chunk, kind).wait()
        multiply(chunk, other_start, other)
        part = other[...]
        top = jnp.maximum(jnp.max(jnp.abs(part), axis=0, keepdims=True), 1e-30)
        code[chunk] = jnp.floor(part * (32766.0 / top) + 0.5).astype(jnp.int16)
        scale[chunk] = jnp.broadcast_to(top * (1.0 / 32766.0), scale.shape[1:])
        code_copy(chunk).start()
        scale_copy(chunk).start()
        multiply(chunk, own_start, own.at[chunk])

        @pl.when(chunk >= LAG)
        def _():
            finish(chunk - LAG)

        return carry

    for load in load_state:
        load.wait()
    lax.fori_loop(0, chunks, work, 0)

    def finish_rest(chunk, carry):
        finish(chunk)
        return carry

    lax.fori_loop(chunks - LAG, chunks, finish_rest, 0)

    over_all_pipes.wait_recv()
    over_out[...] = jnp.max(over_pipe[...], axis=0)
    send_routes.wait_send()
    over_all_plane.wait_send()
    over_to_partner.wait_send()
    over_all_pipes.wait_send()

    def drain(chunk, carry):
        for kind in range(2):
            all_blocks(chunk, kind).wait_send()
        packed_copy(chunk).wait_send()
        code_copy(chunk).wait_send()
        scale_copy(chunk).wait_send()
        return carry

    lax.fori_loop(0, chunks, drain, 0)


def store_kernel(*refs):
    count = len(refs) // 2
    sems = refs[-1]
    copies = [
        pltpu.make_async_copy(refs[i], refs[count + i].at[0, 0], sems.at[i]) for i in range(count)
    ]
    for copy in copies:
        copy.start()
    for copy in copies:
        copy.wait()


def body(out_grad, routes, saved_hidden, master, moment1, moment2):
    expert_count = lax.axis_size("expert")
    slots, width = out_grad.shape
    cap, hid = saved_hidden.shape[3:]
    half, cols = master.shape[2:]
    chunks = cols // LANE
    bf16, f32 = jnp.bfloat16, jnp.float32
    dma = pltpu.SemaphoreType.DMA
    split, plane = expert_count // EXPG, expert_count // 2
    state = pltpu.VMEM((half, cols), f32)
    operands = (
        out_grad, pltpu.with_memory_space_constraint(routes.reshape(1, slots), pltpu.HBM), saved_hidden,
        master, moment1, moment2,
    )

    def every_row():
        states = pl.pallas_call(
            exchange_kernel,
            out_shape=(state, state, state),
            in_specs=[
                pl.BlockSpec(memory_space=pl.ANY),
                pl.BlockSpec(memory_space=pltpu.HBM),
                pl.BlockSpec(memory_space=pl.ANY),
                pl.BlockSpec(memory_space=pl.ANY),
                pl.BlockSpec(memory_space=pl.ANY),
                pl.BlockSpec(memory_space=pl.ANY),
            ],
            out_specs=[pl.BlockSpec(memory_space=pltpu.VMEM)] * 3,
            scratch_shapes=[
                pltpu.VMEM((slots, width), bf16),
                pltpu.VMEM((1, slots), jnp.int32),
                pltpu.VMEM((EXPG * cap, slots), bf16),
                pltpu.VMEM((chunks, expert_count, cap, LANE), bf16),
                pltpu.VMEM((chunks, expert_count, cap, LANE), bf16),
                pltpu.VMEM((expert_count, cap, hid), bf16),
                pltpu.VMEM((hid, expert_count * cap), bf16),
                pltpu.VMEM((chunks, half, LANE), f32),
                pltpu.VMEM((half, LANE), f32),
                pltpu.VMEM((chunks, half, LANE), jnp.int16),
                pltpu.VMEM((chunks, half, LANE), jnp.int16),
                pltpu.VMEM((chunks, 8, LANE), f32),
                pltpu.VMEM((chunks, 8, LANE), f32),
                dma((6,)),
            ] + [dma((chunks,))] * 7,
            compiler_params=pltpu.CompilerParams(
                collective_id=1, has_side_effects=True, vmem_limit_bytes=48 * 1024 * 1024
            ),
            cost_estimate=pl.CostEstimate(
                flops=2 * expert_count * cap * hid * cols, bytes_accessed=16 << 20, transcendentals=0
            ),
            name="exchange",
        )(*operands)
        return stored(states)

    def stored(states):
        shape = jax.ShapeDtypeStruct((1, 1, half, cols), f32)
        return pl.pallas_call(
            store_kernel,
            out_shape=(shape, shape, shape),
            in_specs=[pl.BlockSpec(memory_space=pltpu.VMEM)] * 3,
            out_specs=[pl.BlockSpec(memory_space=pl.ANY)] * 3,
            scratch_shapes=[dma((3,))],
            compiler_params=pltpu.CompilerParams(vmem_limit_bytes=1024 * 1024),
            name="store",
        )(*(pltpu.with_memory_space_constraint(new, pltpu.VMEM) for new in states))

    *states, over = pl.pallas_call(
        relay_kernel,
        out_shape=(state, state, state, jax.ShapeDtypeStruct((8, LANE), jnp.int32)),
        in_specs=[pl.BlockSpec(memory_space=pl.ANY), pl.BlockSpec(memory_space=pltpu.HBM)]
        + [pl.BlockSpec(memory_space=pl.ANY)] * 4,
        out_specs=[pl.BlockSpec(memory_space=pltpu.VMEM)] * 4,
        scratch_shapes=[
            pltpu.VMEM((slots, width), bf16),
            pltpu.VMEM((1, slots), jnp.int32),
            pltpu.VMEM((1, slots), jnp.int32),
            pltpu.VMEM((EXPG // 2 * cap, slots), bf16),
            pltpu.VMEM((CROSSING, slots), bf16),
            pltpu.VMEM((EXPG // 2 * cap, CROSSING), bf16),
            pltpu.VMEM((chunks, split, CROSSING, LANE), bf16),
            pltpu.VMEM((chunks, split, CROSSING, LANE), bf16),
            pltpu.VMEM((chunks, 2, plane, cap, LANE), bf16),
            pltpu.VMEM((chunks, expert_count, cap, LANE), bf16),
            pltpu.VMEM((2, expert_count // 8, cap, hid), bf16),
            pltpu.VMEM((hid, expert_count * cap), bf16),
            pltpu.VMEM((chunks, half, LANE), f32),
            pltpu.VMEM((half, LANE), f32),
            pltpu.VMEM((chunks, half, LANE), jnp.int16),
            pltpu.VMEM((chunks, half, LANE), jnp.int16),
            pltpu.VMEM((chunks, 8, LANE), f32),
            pltpu.VMEM((chunks, 8, LANE), f32),
            pltpu.VMEM((plane, 8, LANE), jnp.int32),
            pltpu.VMEM((2, 8, LANE), jnp.int32),
            pltpu.VMEM((lax.axis_size("pipe"), 8, LANE), jnp.int32),
            dma((5,)),
            dma((2,)),
            dma((2,)),
            dma((6,)),
            dma((chunks,)),
            dma((chunks,)),
            dma((2, chunks)),
            dma((2, chunks)),
            dma((2, chunks)),
        ] + [dma((chunks,))] * 4,
        compiler_params=pltpu.CompilerParams(
            collective_id=0, has_side_effects=True, vmem_limit_bytes=48 * 1024 * 1024
        ),
        cost_estimate=pl.CostEstimate(
            flops=2 * expert_count * cap * hid * cols, bytes_accessed=16 << 20, transcendentals=0
        ),
        name="relay",
    )(*operands)
    done = stored(states)
    return lax.cond(over[0, 0] > 0, every_row, lambda: done)


def solution(mesh):
    in_specs = (
        P(("pipe", "expert"), None),
        P(("pipe", "expert"), None),
        P("pipe", "expert", None, None, None),
        P("pipe", "expert", None, None),
        P("pipe", "expert", None, None),
        P("pipe", "expert", None, None),
    )
    out_specs = (
        P("pipe", "expert", None, None),
        P("pipe", "expert", None, None),
        P("pipe", "expert", None, None),
    )
    return jax.shard_map(body, mesh=mesh, in_specs=in_specs, out_specs=out_specs, check_vma=False)
```

```python
import jax
import jax.numpy as jnp
from jax import lax
from jax.experimental import pallas as pl
from jax.experimental.pallas import tpu as pltpu
from jax.sharding import PartitionSpec as P

EXPG = 4
LANE = 128
LAG = 3
FIRST = 4
BEHIND = 2
CROSSING = 208
MESH = pl.DeviceIdType.MESH


def exchange_kernel(
    grad_hbm, routes_hbm, hidden_hbm, master_hbm, moment1_hbm, moment2_hbm, master, moment1, moment2,
    grad, routes, place, outbound, arrived, hidden, hidden_t, own, other, code, code_in, scale, scale_in,
    load_sem, local_sem, send_sem, recv_sem, code_send, code_recv, scale_send, scale_recv,
):
    pipe, me = lax.axis_index("pipe"), lax.axis_index("expert")
    pipe_count, expert_count = lax.axis_size("pipe"), lax.axis_size("expert")
    chunks, _, cap, _ = outbound.shape
    slots, width = grad.shape
    split = expert_count // EXPG
    slab = width // split
    hid = hidden_t.shape[0]
    half = hid // 2
    mirror = pipe_count - 1 - pipe
    keep_high = pipe // (pipe_count // 2)
    own_start = pl.multiple_of(keep_high * half, half)
    other_start = pl.multiple_of((1 - keep_high) * half, half)
    tile = half // 2

    load_grad = pltpu.make_async_copy(grad_hbm, grad, load_sem.at[0])
    load_grad.start()
    load_routes = pltpu.make_async_copy(routes_hbm, routes, load_sem.at[5])
    load_routes.start()
    load_hidden = pltpu.make_async_copy(hidden_hbm.at[0, 0], hidden, load_sem.at[1])
    load_hidden.start()
    load_state = [
        pltpu.make_async_copy(src.at[0, 0], dst, load_sem.at[2 + i])
        for i, (src, dst) in enumerate(((master_hbm, master), (moment1_hbm, moment1), (moment2_hbm, moment2)))
    ]
    for load in load_state:
        load.start()

    barrier = pltpu.get_barrier_semaphore()

    def greet(step, carry):
        pl.semaphore_signal(
            barrier, inc=1, device_id=(pipe, lax.rem(me + step, expert_count)), device_id_type=MESH
        )
        return carry

    lax.fori_loop(1, expert_count, greet, 0)
    pl.semaphore_signal(barrier, inc=1, device_id=(mirror, me), device_id_type=MESH)

    load_routes.wait()
    route = routes[...]
    chosen = jnp.broadcast_to(route, (8, slots)) == lax.broadcasted_iota(jnp.int32, (8, slots), 0)
    earlier = lax.broadcasted_iota(jnp.int32, (slots, slots), 0) < lax.broadcasted_iota(jnp.int32, (slots, slots), 1)
    before = jnp.dot(
        chosen.astype(jnp.bfloat16), earlier.astype(jnp.bfloat16), preferred_element_type=jnp.float32
    )
    rank = jnp.sum(jnp.where(chosen, before, 0.0), axis=0, keepdims=True).astype(jnp.int32)
    flat = jnp.broadcast_to(route * cap + rank, (EXPG * cap, slots))
    placed = flat == lax.broadcasted_iota(jnp.int32, (EXPG * cap, slots), 0)
    place[...] = placed.astype(jnp.bfloat16)

    load_grad.wait()

    def block(chunk, peer):
        return pltpu.make_async_remote_copy(
            src_ref=outbound.at[chunk, peer],
            dst_ref=arrived.at[chunk, me],
            send_sem=send_sem.at[chunk],
            recv_sem=recv_sem.at[chunk],
            device_id=(pipe, peer),
            device_id_type=MESH,
        )

    def local(chunk):
        return pltpu.make_async_copy(outbound.at[chunk, me], arrived.at[chunk, me], local_sem.at[chunk])

    def pick_send(chunk, carry):
        for step in range(split):
            j = lax.rem(me + step, split)
            start = pl.multiple_of(j * slab + chunk * LANE, LANE)
            picked = jnp.dot(place[...], grad[:, pl.ds(start, LANE)], preferred_element_type=jnp.float32)
            picked = picked.astype(jnp.bfloat16)
            for k in range(EXPG):
                outbound[chunk, k * split + j] = picked[k * cap:(k + 1) * cap]
            for turn_k in range(EXPG):
                k = lax.rem(me // split + EXPG - 1 - turn_k, EXPG)
                if step == 0 and turn_k == EXPG - 1:
                    local(chunk).start()
                else:
                    block(chunk, k * split + j).start()
        return carry

    def all_blocks(chunk):
        others = pl.ds(0, expert_count - 1)
        return pltpu.make_async_remote_copy(
            src_ref=outbound.at[chunk, others],
            dst_ref=arrived.at[chunk, others],
            send_sem=send_sem.at[chunk],
            recv_sem=recv_sem.at[chunk],
            device_id=(pipe, me),
            device_id_type=MESH,
        )

    pl.semaphore_wait(barrier, expert_count)
    lax.fori_loop(0, chunks, pick_send, 0)

    load_hidden.wait()

    def turn(s, carry):
        at = pl.multiple_of(s * cap, cap)
        hidden_t[:, pl.ds(at, cap)] = hidden[s].T
        return carry

    lax.fori_loop(0, expert_count, turn, 0)

    def code_copy(chunk):
        return pltpu.make_async_remote_copy(
            src_ref=code.at[chunk], dst_ref=code_in.at[chunk],
            send_sem=code_send.at[chunk], recv_sem=code_recv.at[chunk],
            device_id=(mirror, me), device_id_type=MESH,
        )

    def scale_copy(chunk):
        return pltpu.make_async_remote_copy(
            src_ref=scale.at[chunk], dst_ref=scale_in.at[chunk],
            send_sem=scale_send.at[chunk], recv_sem=scale_recv.at[chunk],
            device_id=(mirror, me), device_id_type=MESH,
        )

    def multiply(chunk, first, into):
        def one(i, carry):
            row = pl.multiple_of(i * tile, tile)
            rows = pl.ds(pl.multiple_of(first + row, tile), tile)
            cols = arrived[chunk].reshape(expert_count * cap, LANE)
            into[pl.ds(row, tile), :] = jnp.dot(hidden_t[rows, :], cols, preferred_element_type=jnp.float32)
            return carry

        lax.fori_loop(0, half // tile, one, 0)

    def finish(chunk):
        code_copy(chunk).wait_recv()
        scale_copy(chunk).wait_recv()
        summed = own[chunk] + code_in[chunk].astype(jnp.float32) * scale_in[chunk, 0:1, :]
        cols = pl.ds(pl.multiple_of(chunk * LANE, LANE), LANE)
        new_moment1 = 0.9 * moment1[:, cols] + 0.1 * summed
        new_moment2 = 0.95 * moment2[:, cols] + 0.05 * summed * summed
        weight = master[:, cols]
        update = new_moment1 / (1.0 - 0.9**10) / (jnp.sqrt(new_moment2 / (1.0 - 0.95**10)) + 1e-08)
        master[:, cols] = weight - 0.2 * (update + 0.05 * weight)
        moment1[:, cols] = new_moment1
        moment2[:, cols] = new_moment2

    def work(chunk, carry):
        all_blocks(chunk).wait_recv()
        local(chunk).wait()
        multiply(chunk, other_start, other)
        part = other[...]
        top = jnp.maximum(jnp.max(jnp.abs(part), axis=0, keepdims=True), 1e-30)
        code[chunk] = jnp.floor(part * (32766.0 / top) + 0.5).astype(jnp.int16)
        scale[chunk] = jnp.broadcast_to(top * (1.0 / 32766.0), scale.shape[1:])
        code_copy(chunk).start()
        scale_copy(chunk).start()
        multiply(chunk, own_start, own.at[chunk])

        @pl.when(chunk >= LAG)
        def _():
            finish(chunk - LAG)

        return carry

    for load in load_state:
        load.wait()
    lax.fori_loop(0, chunks, work, 0)

    def finish_rest(chunk, carry):
        finish(chunk)
        return carry

    lax.fori_loop(chunks - LAG, chunks, finish_rest, 0)

    def drain(chunk, carry):
        all_blocks(chunk).wait_send()
        code_copy(chunk).wait_send()
        scale_copy(chunk).wait_send()
        return carry

    lax.fori_loop(0, chunks, drain, 0)


def relay_kernel(
    grad_hbm, routes_hbm, hidden_hbm, master_hbm, moment1_hbm, moment2_hbm, master, moment1, moment2, over_out,
    grad, routes, routes_in, place, pack, expand, packed, packed_in, outbound, arrived, hidden, hidden_t,
    own, other, code, code_in, scale, scale_in, over_plane, over_pair, over_pipe,
    load_sem, hidden_sem, routes_sem, over_sem, pack_send, pack_recv, local_sem, send_sem, recv_sem,
    code_send, code_recv, scale_send, scale_recv,
):
    pipe, me = lax.axis_index("pipe"), lax.axis_index("expert")
    pipe_count, expert_count = lax.axis_size("pipe"), lax.axis_size("expert")
    chunks, _, plane, cap, _ = outbound.shape
    slots, width = grad.shape
    split = expert_count // EXPG
    slab = width // split
    hid = hidden_t.shape[0]
    half = hid // 2
    mirror = pipe_count - 1 - pipe
    keep_high = pipe // (pipe_count // 2)
    own_start = pl.multiple_of(keep_high * half, half)
    other_start = pl.multiple_of((1 - keep_high) * half, half)
    tile = half // 2
    side = me // plane
    seat = me % plane
    base = side * plane
    partner = lax.rem(me + plane, expert_count)
    local_experts = EXPG // 2
    bound = packed.shape[2]

    load_routes = pltpu.make_async_copy(routes_hbm, routes, load_sem.at[0])
    load_routes.start()
    load_grad = pltpu.make_async_copy(grad_hbm, grad, load_sem.at[1])
    load_grad.start()
    group = hidden.shape[1]

    def load_hidden(turn):
        return pltpu.make_async_copy(
            hidden_hbm.at[0, 0, pl.ds(turn * group, group)], hidden.at[turn % 2], hidden_sem.at[turn % 2]
        )

    load_hidden(0).start()
    load_hidden(1).start()
    load_state = [
        pltpu.make_async_copy(src.at[0, 0], dst, load_sem.at[2 + i])
        for i, (src, dst) in enumerate(((master_hbm, master), (moment1_hbm, moment1), (moment2_hbm, moment2)))
    ]
    for load in load_state:
        load.start()

    barrier = pltpu.get_barrier_semaphore()

    def greet(step, carry):
        pl.semaphore_signal(
            barrier, inc=1, device_id=(pipe, base + lax.rem(seat + step, plane)), device_id_type=MESH
        )
        return carry

    lax.fori_loop(1, plane, greet, 0)
    pl.semaphore_signal(barrier, inc=1, device_id=(pipe, partner), device_id_type=MESH)
    for step in range(1, pipe_count):
        pl.semaphore_signal(barrier, inc=1, device_id=(lax.rem(pipe + step, pipe_count), me), device_id_type=MESH)

    def one_hots(route, packed_side):
        expert = lax.broadcasted_iota(jnp.int32, (8, slots), 0)
        chosen = jnp.broadcast_to(route, (8, slots)) == expert
        earlier = lax.broadcasted_iota(jnp.int32, (slots, slots), 0) < lax.broadcasted_iota(jnp.int32, (slots, slots), 1)
        before = jnp.dot(
            chosen.astype(jnp.bfloat16), earlier.astype(jnp.bfloat16), preferred_element_type=jnp.float32
        )
        rank = jnp.sum(jnp.where(chosen, before, 0.0), axis=0, keepdims=True).astype(jnp.int32)
        flat = jnp.broadcast_to((route - side * local_experts) * cap + rank, (local_experts * cap, slots))
        places = flat == lax.broadcasted_iota(jnp.int32, (local_experts * cap, slots), 0)
        first = packed_side * local_experts
        in_side = (expert >= first) & (expert < first + local_experts)
        order = jnp.sum(jnp.where(in_side, before, 0.0), axis=0, keepdims=True).astype(jnp.int32)
        goes = (route >= first) & (route < first + local_experts)
        order = jnp.broadcast_to(jnp.where(goes, order, -1), (bound, slots))
        ranks = order == lax.broadcasted_iota(jnp.int32, (bound, slots), 0)
        return places.astype(jnp.bfloat16), ranks.astype(jnp.bfloat16), goes

    load_routes.wait()
    own_places, own_ranks, goes = one_hots(routes[...], 1 - side)
    place[...] = own_places
    pack[...] = own_ranks
    crossing = jnp.sum(goes.astype(jnp.float32), axis=1, keepdims=True)
    over = jnp.broadcast_to((crossing > bound).astype(jnp.int32), over_pair.shape[1:])
    over_plane[seat] = over

    load_grad.wait()
    pl.semaphore_wait(barrier, plane - 1 + 1 + pipe_count - 1)

    send_routes = pltpu.make_async_remote_copy(
        src_ref=routes, dst_ref=routes_in, send_sem=routes_sem.at[0], recv_sem=routes_sem.at[1],
        device_id=(pipe, partner), device_id_type=MESH,
    )
    send_routes.start()

    def over_to_plane(seat_to):
        return pltpu.make_async_remote_copy(
            src_ref=over_plane.at[seat], dst_ref=over_plane.at[seat],
            send_sem=over_sem.at[0], recv_sem=over_sem.at[1],
            device_id=(pipe, base + seat_to), device_id_type=MESH,
        )

    def tell_plane(step, carry):
        over_to_plane(lax.rem(seat + step, plane)).start()
        return carry

    over_all_plane = pltpu.make_async_remote_copy(
        src_ref=over_plane.at[pl.ds(0, plane - 1)], dst_ref=over_plane.at[pl.ds(0, plane - 1)],
        send_sem=over_sem.at[0], recv_sem=over_sem.at[1],
        device_id=(pipe, partner), device_id_type=MESH,
    )
    over_to_partner = pltpu.make_async_remote_copy(
        src_ref=over_pair.at[0], dst_ref=over_pair.at[1],
        send_sem=over_sem.at[2], recv_sem=over_sem.at[3],
        device_id=(pipe, partner), device_id_type=MESH,
    )
    over_to_pipes = [
        pltpu.make_async_remote_copy(
            src_ref=over_pipe.at[pipe], dst_ref=over_pipe.at[pipe],
            send_sem=over_sem.at[4], recv_sem=over_sem.at[5],
            device_id=(lax.rem(pipe + step, pipe_count), me), device_id_type=MESH,
        )
        for step in range(1, pipe_count)
    ]
    over_all_pipes = pltpu.make_async_remote_copy(
        src_ref=over_pipe.at[pl.ds(0, pipe_count - 1)], dst_ref=over_pipe.at[pl.ds(0, pipe_count - 1)],
        send_sem=over_sem.at[4], recv_sem=over_sem.at[5],
        device_id=(mirror, me), device_id_type=MESH,
    )

    def block(chunk, kind, to):
        return pltpu.make_async_remote_copy(
            src_ref=outbound.at[chunk, kind, to],
            dst_ref=arrived.at[chunk, me if kind == 0 else partner],
            send_sem=send_sem.at[kind, chunk],
            recv_sem=recv_sem.at[kind, chunk],
            device_id=(pipe, base + to),
            device_id_type=MESH,
        )

    def local(chunk, kind):
        return pltpu.make_async_copy(
            outbound.at[chunk, kind, seat],
            arrived.at[chunk, me if kind == 0 else partner],
            local_sem.at[kind, chunk],
        )

    def all_blocks(chunk, kind):
        others = pl.ds(0, plane - 1)
        return pltpu.make_async_remote_copy(
            src_ref=outbound.at[chunk, kind, others],
            dst_ref=arrived.at[chunk, others],
            send_sem=send_sem.at[kind, chunk],
            recv_sem=recv_sem.at[kind, chunk],
            device_id=(pipe, partner),
            device_id_type=MESH,
        )

    def spread(chunk, kind, step, j, rows):
        rows = rows.astype(jnp.bfloat16)
        for k in range(local_experts):
            outbound[chunk, kind, k * split + j] = rows[k * cap:(k + 1) * cap]
        for turn in range(local_experts):
            k = lax.rem(seat // split + local_experts - 1 - turn, local_experts)
            if step == 0 and turn == local_experts - 1:
                local(chunk, kind).start()
            else:
                block(chunk, kind, k * split + j).start()

    def slab_cols(chunk, j):
        return pl.ds(pl.multiple_of(j * slab + chunk * LANE, LANE), LANE)

    def packed_copy(chunk, j):
        return pltpu.make_async_remote_copy(
            src_ref=packed.at[chunk, j], dst_ref=packed_in.at[chunk, j],
            send_sem=pack_send.at[chunk], recv_sem=pack_recv.at[chunk],
            device_id=(pipe, partner), device_id_type=MESH,
        )

    def packed_all(chunk):
        return pltpu.make_async_remote_copy(
            src_ref=packed.at[chunk], dst_ref=packed_in.at[chunk],
            send_sem=pack_send.at[chunk], recv_sem=pack_recv.at[chunk],
            device_id=(pipe, partner), device_id_type=MESH,
        )

    def slab_step(step, new, passed):
        j = lax.rem(seat + step, split)
        if passed is not None:
            rows = jnp.dot(expand[...], packed_in[passed, j], preferred_element_type=jnp.float32)
            spread(passed, 1, step, j, rows)
        if new is not None:
            rows = jnp.dot(place[...], grad[:, slab_cols(new, j)], preferred_element_type=jnp.float32)
            spread(new, 0, step, j, rows)
            rows = jnp.dot(pack[...], grad[:, slab_cols(new, j)], preferred_element_type=jnp.float32)
            packed[new, j] = rows.astype(jnp.bfloat16)
            packed_copy(new, j).start()

    def first_sends(chunk, carry):
        for step in range(split):
            slab_step(step, chunk, None)
        return carry

    first_sends(0, 0)
    lax.fori_loop(1, plane, tell_plane, 0)
    lax.fori_loop(1, FIRST, first_sends, 0)

    send_routes.wait_recv()
    their_places, their_ranks, _ = one_hots(routes_in[...], side)
    expand[...] = lax.dot_general(
        their_places, their_ranks, (((1,), (1,)), ((), ())), preferred_element_type=jnp.float32
    ).astype(jnp.bfloat16)

    turns = expert_count // group

    def flip_turn(turn, carry):
        load_hidden(turn).wait()

        def flip(i, carry):
            at = pl.multiple_of((turn * group + i) * cap, cap)
            hidden_t[:, pl.ds(at, cap)] = hidden[turn % 2, i].T
            return carry

        lax.fori_loop(0, group, flip, 0)

        @pl.when(turn + 2 < turns)
        def _():
            load_hidden(turn + 2).start()

        return carry

    def code_copy(chunk):
        return pltpu.make_async_remote_copy(
            src_ref=code.at[chunk], dst_ref=code_in.at[chunk],
            send_sem=code_send.at[chunk], recv_sem=code_recv.at[chunk],
            device_id=(mirror, me), device_id_type=MESH,
        )

    def scale_copy(chunk):
        return pltpu.make_async_remote_copy(
            src_ref=scale.at[chunk], dst_ref=scale_in.at[chunk],
            send_sem=scale_send.at[chunk], recv_sem=scale_recv.at[chunk],
            device_id=(mirror, me), device_id_type=MESH,
        )

    def multiply(chunk, first, into):
        def one(i, carry):
            row = pl.multiple_of(i * tile, tile)
            rows = pl.ds(pl.multiple_of(first + row, tile), tile)
            cols = arrived[chunk].reshape(expert_count * cap, LANE)
            into[pl.ds(row, tile), :] = jnp.dot(hidden_t[rows, :], cols, preferred_element_type=jnp.float32)
            return carry

        lax.fori_loop(0, half // tile, one, 0)

    def finish(chunk):
        code_copy(chunk).wait_recv()
        scale_copy(chunk).wait_recv()
        summed = own[chunk] + code_in[chunk].astype(jnp.float32) * scale_in[chunk, 0:1, :]
        cols = pl.ds(pl.multiple_of(chunk * LANE, LANE), LANE)
        new_moment1 = 0.9 * moment1[:, cols] + 0.1 * summed
        new_moment2 = 0.95 * moment2[:, cols] + 0.05 * summed * summed
        weight = master[:, cols]
        update = new_moment1 / (1.0 - 0.9**10) / (jnp.sqrt(new_moment2 / (1.0 - 0.95**10)) + 1e-08)
        master[:, cols] = weight - 0.2 * (update + 0.05 * weight)
        moment1[:, cols] = new_moment1
        moment2[:, cols] = new_moment2

    def work(chunk, carry):
        for kind in range(2):
            all_blocks(chunk, kind).wait_recv()
            local(chunk, kind).wait()
        multiply(chunk, other_start, other)
        part = other[...]
        top = jnp.maximum(jnp.max(jnp.abs(part), axis=0, keepdims=True), 1e-30)
        code[chunk] = jnp.floor(part * (32766.0 / top) + 0.5).astype(jnp.int16)
        scale[chunk] = jnp.broadcast_to(top * (1.0 / 32766.0), scale.shape[1:])
        code_copy(chunk).start()
        scale_copy(chunk).start()
        multiply(chunk, own_start, own.at[chunk])

        @pl.when(chunk >= LAG)
        def _():
            finish(chunk - LAG)

        return carry

    for load in load_state:
        load.wait()

    def both(chunk, carry):
        packed_all(chunk).wait_recv()
        for step in range(split):
            slab_step(step, chunk + FIRST, chunk)

        @pl.when(chunk < BEHIND)
        def _():
            lax.fori_loop(chunk * turns // BEHIND, (chunk + 1) * turns // BEHIND, flip_turn, 0)

        @pl.when(chunk >= BEHIND)
        def _():
            work(chunk - BEHIND, 0)

        return carry

    def passing(chunk, carry):
        packed_all(chunk).wait_recv()
        for step in range(split):
            slab_step(step, None, chunk)
        work(chunk - BEHIND, 0)
        return carry

    lax.fori_loop(0, chunks - FIRST, both, 0)

    over_all_plane.wait_recv()
    over_pair[0] = jnp.max(over_plane[...], axis=0)
    over_to_partner.start()

    lax.fori_loop(chunks - FIRST, chunks, passing, 0)

    over_to_partner.wait_recv()
    over_pipe[pipe] = jnp.maximum(over_pair[0], over_pair[1])
    for copy in over_to_pipes:
        copy.start()

    lax.fori_loop(chunks - BEHIND, chunks, work, 0)

    def finish_rest(chunk, carry):
        finish(chunk)
        return carry

    lax.fori_loop(chunks - LAG, chunks, finish_rest, 0)

    over_all_pipes.wait_recv()
    over_out[...] = jnp.max(over_pipe[...], axis=0)
    send_routes.wait_send()
    over_all_plane.wait_send()
    over_to_partner.wait_send()
    over_all_pipes.wait_send()

    def drain(chunk, carry):
        for kind in range(2):
            all_blocks(chunk, kind).wait_send()
        packed_all(chunk).wait_send()
        code_copy(chunk).wait_send()
        scale_copy(chunk).wait_send()
        return carry

    lax.fori_loop(0, chunks, drain, 0)


def store_kernel(*refs):
    count = len(refs) // 2
    sems = refs[-1]
    copies = [
        pltpu.make_async_copy(refs[i], refs[count + i].at[0, 0], sems.at[i]) for i in range(count)
    ]
    for copy in copies:
        copy.start()
    for copy in copies:
        copy.wait()


def body(out_grad, routes, saved_hidden, master, moment1, moment2):
    expert_count = lax.axis_size("expert")
    slots, width = out_grad.shape
    cap, hid = saved_hidden.shape[3:]
    half, cols = master.shape[2:]
    chunks = cols // LANE
    bf16, f32 = jnp.bfloat16, jnp.float32
    dma = pltpu.SemaphoreType.DMA
    split, plane = expert_count // EXPG, expert_count // 2
    state = pltpu.VMEM((half, cols), f32)
    operands = (
        out_grad, pltpu.with_memory_space_constraint(routes.reshape(1, slots), pltpu.HBM), saved_hidden,
        master, moment1, moment2,
    )

    def every_row():
        states = pl.pallas_call(
            exchange_kernel,
            out_shape=(state, state, state),
            in_specs=[
                pl.BlockSpec(memory_space=pl.ANY),
                pl.BlockSpec(memory_space=pltpu.HBM),
                pl.BlockSpec(memory_space=pl.ANY),
                pl.BlockSpec(memory_space=pl.ANY),
                pl.BlockSpec(memory_space=pl.ANY),
                pl.BlockSpec(memory_space=pl.ANY),
            ],
            out_specs=[pl.BlockSpec(memory_space=pltpu.VMEM)] * 3,
            scratch_shapes=[
                pltpu.VMEM((slots, width), bf16),
                pltpu.VMEM((1, slots), jnp.int32),
                pltpu.VMEM((EXPG * cap, slots), bf16),
                pltpu.VMEM((chunks, expert_count, cap, LANE), bf16),
                pltpu.VMEM((chunks, expert_count, cap, LANE), bf16),
                pltpu.VMEM((expert_count, cap, hid), bf16),
                pltpu.VMEM((hid, expert_count * cap), bf16),
                pltpu.VMEM((chunks, half, LANE), f32),
                pltpu.VMEM((half, LANE), f32),
                pltpu.VMEM((chunks, half, LANE), jnp.int16),
                pltpu.VMEM((chunks, half, LANE), jnp.int16),
                pltpu.VMEM((chunks, 8, LANE), f32),
                pltpu.VMEM((chunks, 8, LANE), f32),
                dma((6,)),
            ] + [dma((chunks,))] * 7,
            compiler_params=pltpu.CompilerParams(
                collective_id=1, has_side_effects=True, vmem_limit_bytes=48 * 1024 * 1024
            ),
            cost_estimate=pl.CostEstimate(
                flops=2 * expert_count * cap * hid * cols, bytes_accessed=16 << 20, transcendentals=0
            ),
            name="exchange",
        )(*operands)
        return stored(states)

    def stored(states):
        shape = jax.ShapeDtypeStruct((1, 1, half, cols), f32)
        return pl.pallas_call(
            store_kernel,
            out_shape=(shape, shape, shape),
            in_specs=[pl.BlockSpec(memory_space=pltpu.VMEM)] * 3,
            out_specs=[pl.BlockSpec(memory_space=pl.ANY)] * 3,
            scratch_shapes=[dma((3,))],
            compiler_params=pltpu.CompilerParams(vmem_limit_bytes=1024 * 1024),
            name="store",
        )(*(pltpu.with_memory_space_constraint(new, pltpu.VMEM) for new in states))

    *states, over = pl.pallas_call(
        relay_kernel,
        out_shape=(state, state, state, jax.ShapeDtypeStruct((8, LANE), jnp.int32)),
        in_specs=[pl.BlockSpec(memory_space=pl.ANY), pl.BlockSpec(memory_space=pltpu.HBM)]
        + [pl.BlockSpec(memory_space=pl.ANY)] * 4,
        out_specs=[pl.BlockSpec(memory_space=pltpu.VMEM)] * 4,
        scratch_shapes=[
            pltpu.VMEM((slots, width), bf16),
            pltpu.VMEM((1, slots), jnp.int32),
            pltpu.VMEM((1, slots), jnp.int32),
            pltpu.VMEM((EXPG // 2 * cap, slots), bf16),
            pltpu.VMEM((CROSSING, slots), bf16),
            pltpu.VMEM((EXPG // 2 * cap, CROSSING), bf16),
            pltpu.VMEM((chunks, split, CROSSING, LANE), bf16),
            pltpu.VMEM((chunks, split, CROSSING, LANE), bf16),
            pltpu.VMEM((chunks, 2, plane, cap, LANE), bf16),
            pltpu.VMEM((chunks, expert_count, cap, LANE), bf16),
            pltpu.VMEM((2, expert_count // 8, cap, hid), bf16),
            pltpu.VMEM((hid, expert_count * cap), bf16),
            pltpu.VMEM((chunks, half, LANE), f32),
            pltpu.VMEM((half, LANE), f32),
            pltpu.VMEM((chunks, half, LANE), jnp.int16),
            pltpu.VMEM((chunks, half, LANE), jnp.int16),
            pltpu.VMEM((chunks, 8, LANE), f32),
            pltpu.VMEM((chunks, 8, LANE), f32),
            pltpu.VMEM((plane, 8, LANE), jnp.int32),
            pltpu.VMEM((2, 8, LANE), jnp.int32),
            pltpu.VMEM((lax.axis_size("pipe"), 8, LANE), jnp.int32),
            dma((5,)),
            dma((2,)),
            dma((2,)),
            dma((6,)),
            dma((chunks,)),
            dma((chunks,)),
            dma((2, chunks)),
            dma((2, chunks)),
            dma((2, chunks)),
        ] + [dma((chunks,))] * 4,
        compiler_params=pltpu.CompilerParams(
            collective_id=0, has_side_effects=True, vmem_limit_bytes=48 * 1024 * 1024
        ),
        cost_estimate=pl.CostEstimate(
            flops=2 * expert_count * cap * hid * cols, bytes_accessed=16 << 20, transcendentals=0
        ),
        name="relay",
    )(*operands)
    done = stored(states)
    return lax.cond(over[0, 0] > 0, every_row, lambda: done)


def solution(mesh):
    in_specs = (
        P(("pipe", "expert"), None),
        P(("pipe", "expert"), None),
        P("pipe", "expert", None, None, None),
        P("pipe", "expert", None, None),
        P("pipe", "expert", None, None),
        P("pipe", "expert", None, None),
    )
    out_specs = (
        P("pipe", "expert", None, None),
        P("pipe", "expert", None, None),
        P("pipe", "expert", None, None),
    )
    return jax.shard_map(body, mesh=mesh, in_specs=in_specs, out_specs=out_specs, check_vma=False)
```

```python
import jax
import jax.numpy as jnp
from jax import lax
from jax.experimental import pallas as pl
from jax.experimental.pallas import tpu as pltpu
from jax.sharding import PartitionSpec as P

EXPG = 4
LANE = 128
LAG = 3
FIRST = 5
BEHIND = 2
CROSSING = 208
MESH = pl.DeviceIdType.MESH


def exchange_kernel(
    grad_hbm, routes_hbm, hidden_hbm, master_hbm, moment1_hbm, moment2_hbm, master, moment1, moment2,
    grad, routes, place, outbound, arrived, hidden, hidden_t, own, other, code, code_in, scale, scale_in,
    load_sem, local_sem, send_sem, recv_sem, code_send, code_recv, scale_send, scale_recv,
):
    pipe, me = lax.axis_index("pipe"), lax.axis_index("expert")
    pipe_count, expert_count = lax.axis_size("pipe"), lax.axis_size("expert")
    chunks, _, cap, _ = outbound.shape
    slots, width = grad.shape
    split = expert_count // EXPG
    slab = width // split
    hid = hidden_t.shape[0]
    half = hid // 2
    mirror = pipe_count - 1 - pipe
    keep_high = pipe // (pipe_count // 2)
    own_start = pl.multiple_of(keep_high * half, half)
    other_start = pl.multiple_of((1 - keep_high) * half, half)
    tile = half // 2

    load_grad = pltpu.make_async_copy(grad_hbm, grad, load_sem.at[0])
    load_grad.start()
    load_routes = pltpu.make_async_copy(routes_hbm, routes, load_sem.at[5])
    load_routes.start()
    load_hidden = pltpu.make_async_copy(hidden_hbm.at[0, 0], hidden, load_sem.at[1])
    load_hidden.start()
    load_state = [
        pltpu.make_async_copy(src.at[0, 0], dst, load_sem.at[2 + i])
        for i, (src, dst) in enumerate(((master_hbm, master), (moment1_hbm, moment1), (moment2_hbm, moment2)))
    ]
    for load in load_state:
        load.start()

    barrier = pltpu.get_barrier_semaphore()

    def greet(step, carry):
        pl.semaphore_signal(
            barrier, inc=1, device_id=(pipe, lax.rem(me + step, expert_count)), device_id_type=MESH
        )
        return carry

    lax.fori_loop(1, expert_count, greet, 0)
    pl.semaphore_signal(barrier, inc=1, device_id=(mirror, me), device_id_type=MESH)

    load_routes.wait()
    route = routes[...]
    chosen = jnp.broadcast_to(route, (8, slots)) == lax.broadcasted_iota(jnp.int32, (8, slots), 0)
    earlier = lax.broadcasted_iota(jnp.int32, (slots, slots), 0) < lax.broadcasted_iota(jnp.int32, (slots, slots), 1)
    before = jnp.dot(
        chosen.astype(jnp.bfloat16), earlier.astype(jnp.bfloat16), preferred_element_type=jnp.float32
    )
    rank = jnp.sum(jnp.where(chosen, before, 0.0), axis=0, keepdims=True).astype(jnp.int32)
    flat = jnp.broadcast_to(route * cap + rank, (EXPG * cap, slots))
    placed = flat == lax.broadcasted_iota(jnp.int32, (EXPG * cap, slots), 0)
    place[...] = placed.astype(jnp.bfloat16)

    load_grad.wait()

    def block(chunk, peer):
        return pltpu.make_async_remote_copy(
            src_ref=outbound.at[chunk, peer],
            dst_ref=arrived.at[chunk, me],
            send_sem=send_sem.at[chunk],
            recv_sem=recv_sem.at[chunk],
            device_id=(pipe, peer),
            device_id_type=MESH,
        )

    def local(chunk):
        return pltpu.make_async_copy(outbound.at[chunk, me], arrived.at[chunk, me], local_sem.at[chunk])

    def pick_send(chunk, carry):
        for step in range(split):
            j = lax.rem(me + step, split)
            start = pl.multiple_of(j * slab + chunk * LANE, LANE)
            picked = jnp.dot(place[...], grad[:, pl.ds(start, LANE)], preferred_element_type=jnp.float32)
            picked = picked.astype(jnp.bfloat16)
            for k in range(EXPG):
                outbound[chunk, k * split + j] = picked[k * cap:(k + 1) * cap]
            for turn_k in range(EXPG):
                k = lax.rem(me // split + EXPG - 1 - turn_k, EXPG)
                if step == 0 and turn_k == EXPG - 1:
                    local(chunk).start()
                else:
                    block(chunk, k * split + j).start()
        return carry

    def all_blocks(chunk):
        others = pl.ds(0, expert_count - 1)
        return pltpu.make_async_remote_copy(
            src_ref=outbound.at[chunk, others],
            dst_ref=arrived.at[chunk, others],
            send_sem=send_sem.at[chunk],
            recv_sem=recv_sem.at[chunk],
            device_id=(pipe, me),
            device_id_type=MESH,
        )

    pl.semaphore_wait(barrier, expert_count)
    lax.fori_loop(0, chunks, pick_send, 0)

    load_hidden.wait()

    def turn(s, carry):
        at = pl.multiple_of(s * cap, cap)
        hidden_t[:, pl.ds(at, cap)] = hidden[s].T
        return carry

    lax.fori_loop(0, expert_count, turn, 0)

    def code_copy(chunk):
        return pltpu.make_async_remote_copy(
            src_ref=code.at[chunk], dst_ref=code_in.at[chunk],
            send_sem=code_send.at[chunk], recv_sem=code_recv.at[chunk],
            device_id=(mirror, me), device_id_type=MESH,
        )

    def scale_copy(chunk):
        return pltpu.make_async_remote_copy(
            src_ref=scale.at[chunk], dst_ref=scale_in.at[chunk],
            send_sem=scale_send.at[chunk], recv_sem=scale_recv.at[chunk],
            device_id=(mirror, me), device_id_type=MESH,
        )

    def multiply(chunk, first, into):
        def one(i, carry):
            row = pl.multiple_of(i * tile, tile)
            rows = pl.ds(pl.multiple_of(first + row, tile), tile)
            cols = arrived[chunk].reshape(expert_count * cap, LANE)
            into[pl.ds(row, tile), :] = jnp.dot(hidden_t[rows, :], cols, preferred_element_type=jnp.float32)
            return carry

        lax.fori_loop(0, half // tile, one, 0)

    def finish(chunk):
        code_copy(chunk).wait_recv()
        scale_copy(chunk).wait_recv()
        summed = own[chunk] + code_in[chunk].astype(jnp.float32) * scale_in[chunk, 0:1, :]
        cols = pl.ds(pl.multiple_of(chunk * LANE, LANE), LANE)
        new_moment1 = 0.9 * moment1[:, cols] + 0.1 * summed
        new_moment2 = 0.95 * moment2[:, cols] + 0.05 * summed * summed
        weight = master[:, cols]
        update = new_moment1 / (1.0 - 0.9**10) / (jnp.sqrt(new_moment2 / (1.0 - 0.95**10)) + 1e-08)
        master[:, cols] = weight - 0.2 * (update + 0.05 * weight)
        moment1[:, cols] = new_moment1
        moment2[:, cols] = new_moment2

    def work(chunk, carry):
        all_blocks(chunk).wait_recv()
        local(chunk).wait()
        multiply(chunk, other_start, other)
        part = other[...]
        top = jnp.maximum(jnp.max(jnp.abs(part), axis=0, keepdims=True), 1e-30)
        code[chunk] = jnp.floor(part * (32766.0 / top) + 0.5).astype(jnp.int16)
        scale[chunk] = jnp.broadcast_to(top * (1.0 / 32766.0), scale.shape[1:])
        code_copy(chunk).start()
        scale_copy(chunk).start()
        multiply(chunk, own_start, own.at[chunk])

        @pl.when(chunk >= LAG)
        def _():
            finish(chunk - LAG)

        return carry

    for load in load_state:
        load.wait()
    lax.fori_loop(0, chunks, work, 0)

    def finish_rest(chunk, carry):
        finish(chunk)
        return carry

    lax.fori_loop(chunks - LAG, chunks, finish_rest, 0)

    def drain(chunk, carry):
        all_blocks(chunk).wait_send()
        code_copy(chunk).wait_send()
        scale_copy(chunk).wait_send()
        return carry

    lax.fori_loop(0, chunks, drain, 0)


def relay_kernel(
    grad_hbm, routes_hbm, hidden_hbm, master_hbm, moment1_hbm, moment2_hbm, master, moment1, moment2, over_out,
    grad, routes, routes_in, place, pack, expand, packed, packed_in, outbound, arrived, hidden, hidden_t,
    own, other, code, code_in, scale, scale_in, over_plane, over_pair, over_pipe,
    load_sem, hidden_sem, routes_sem, over_sem, pack_send, pack_recv, local_sem, send_sem, recv_sem,
    code_send, code_recv, scale_send, scale_recv,
):
    pipe, me = lax.axis_index("pipe"), lax.axis_index("expert")
    pipe_count, expert_count = lax.axis_size("pipe"), lax.axis_size("expert")
    chunks, _, plane, cap, _ = outbound.shape
    slots, width = grad.shape
    split = expert_count // EXPG
    slab = width // split
    hid = hidden_t.shape[0]
    half = hid // 2
    mirror = pipe_count - 1 - pipe
    keep_high = pipe // (pipe_count // 2)
    own_start = pl.multiple_of(keep_high * half, half)
    other_start = pl.multiple_of((1 - keep_high) * half, half)
    tile = half // 2
    side = me // plane
    seat = me % plane
    base = side * plane
    partner = lax.rem(me + plane, expert_count)
    local_experts = EXPG // 2
    bound = packed.shape[2]

    load_routes = pltpu.make_async_copy(routes_hbm, routes, load_sem.at[0])
    load_routes.start()
    load_grad = pltpu.make_async_copy(grad_hbm, grad, load_sem.at[1])
    load_grad.start()
    group = hidden.shape[1]

    def load_hidden(turn):
        return pltpu.make_async_copy(
            hidden_hbm.at[0, 0, pl.ds(turn * group, group)], hidden.at[turn % 2], hidden_sem.at[turn % 2]
        )

    load_state = [
        pltpu.make_async_copy(src.at[0, 0], dst, load_sem.at[2 + i])
        for i, (src, dst) in enumerate(((master_hbm, master), (moment1_hbm, moment1), (moment2_hbm, moment2)))
    ]

    barrier = pltpu.get_barrier_semaphore()

    def greet(step, carry):
        pl.semaphore_signal(
            barrier, inc=1, device_id=(pipe, base + lax.rem(seat + step, plane)), device_id_type=MESH
        )
        return carry

    lax.fori_loop(1, plane, greet, 0)
    pl.semaphore_signal(barrier, inc=1, device_id=(pipe, partner), device_id_type=MESH)
    for step in range(1, pipe_count):
        pl.semaphore_signal(barrier, inc=1, device_id=(lax.rem(pipe + step, pipe_count), me), device_id_type=MESH)

    def one_hots(route, packed_side):
        expert = lax.broadcasted_iota(jnp.int32, (8, slots), 0)
        chosen = jnp.broadcast_to(route, (8, slots)) == expert
        earlier = lax.broadcasted_iota(jnp.int32, (slots, slots), 0) < lax.broadcasted_iota(jnp.int32, (slots, slots), 1)
        before = jnp.dot(
            chosen.astype(jnp.bfloat16), earlier.astype(jnp.bfloat16), preferred_element_type=jnp.float32
        )
        rank = jnp.sum(jnp.where(chosen, before, 0.0), axis=0, keepdims=True).astype(jnp.int32)
        flat = jnp.broadcast_to((route - side * local_experts) * cap + rank, (local_experts * cap, slots))
        places = flat == lax.broadcasted_iota(jnp.int32, (local_experts * cap, slots), 0)
        first = packed_side * local_experts
        in_side = (expert >= first) & (expert < first + local_experts)
        order = jnp.sum(jnp.where(in_side, before, 0.0), axis=0, keepdims=True).astype(jnp.int32)
        goes = (route >= first) & (route < first + local_experts)
        order = jnp.broadcast_to(jnp.where(goes, order, -1), (bound, slots))
        ranks = order == lax.broadcasted_iota(jnp.int32, (bound, slots), 0)
        return places.astype(jnp.bfloat16), ranks.astype(jnp.bfloat16), goes

    load_routes.wait()
    own_places, own_ranks, goes = one_hots(routes[...], 1 - side)
    place[...] = own_places
    pack[...] = own_ranks
    crossing = jnp.sum(goes.astype(jnp.float32), axis=1, keepdims=True)
    over = jnp.broadcast_to((crossing > bound).astype(jnp.int32), over_pair.shape[1:])
    over_plane[seat] = over

    load_grad.wait()
    pl.semaphore_wait(barrier, plane - 1 + 1 + pipe_count - 1)

    send_routes = pltpu.make_async_remote_copy(
        src_ref=routes, dst_ref=routes_in, send_sem=routes_sem.at[0], recv_sem=routes_sem.at[1],
        device_id=(pipe, partner), device_id_type=MESH,
    )
    send_routes.start()

    def over_to_plane(seat_to):
        return pltpu.make_async_remote_copy(
            src_ref=over_plane.at[seat], dst_ref=over_plane.at[seat],
            send_sem=over_sem.at[0], recv_sem=over_sem.at[1],
            device_id=(pipe, base + seat_to), device_id_type=MESH,
        )

    def tell_plane(step, carry):
        over_to_plane(lax.rem(seat + step, plane)).start()
        return carry

    over_all_plane = pltpu.make_async_remote_copy(
        src_ref=over_plane.at[pl.ds(0, plane - 1)], dst_ref=over_plane.at[pl.ds(0, plane - 1)],
        send_sem=over_sem.at[0], recv_sem=over_sem.at[1],
        device_id=(pipe, partner), device_id_type=MESH,
    )
    over_to_partner = pltpu.make_async_remote_copy(
        src_ref=over_pair.at[0], dst_ref=over_pair.at[1],
        send_sem=over_sem.at[2], recv_sem=over_sem.at[3],
        device_id=(pipe, partner), device_id_type=MESH,
    )
    over_to_pipes = [
        pltpu.make_async_remote_copy(
            src_ref=over_pipe.at[pipe], dst_ref=over_pipe.at[pipe],
            send_sem=over_sem.at[4], recv_sem=over_sem.at[5],
            device_id=(lax.rem(pipe + step, pipe_count), me), device_id_type=MESH,
        )
        for step in range(1, pipe_count)
    ]
    over_all_pipes = pltpu.make_async_remote_copy(
        src_ref=over_pipe.at[pl.ds(0, pipe_count - 1)], dst_ref=over_pipe.at[pl.ds(0, pipe_count - 1)],
        send_sem=over_sem.at[4], recv_sem=over_sem.at[5],
        device_id=(mirror, me), device_id_type=MESH,
    )

    def block(chunk, kind, to):
        return pltpu.make_async_remote_copy(
            src_ref=outbound.at[chunk, kind, to],
            dst_ref=arrived.at[chunk, me if kind == 0 else partner],
            send_sem=send_sem.at[kind, chunk],
            recv_sem=recv_sem.at[kind, chunk],
            device_id=(pipe, base + to),
            device_id_type=MESH,
        )

    def local(chunk, kind):
        return pltpu.make_async_copy(
            outbound.at[chunk, kind, seat],
            arrived.at[chunk, me if kind == 0 else partner],
            local_sem.at[kind, chunk],
        )

    def all_blocks(chunk, kind):
        others = pl.ds(0, plane - 1)
        return pltpu.make_async_remote_copy(
            src_ref=outbound.at[chunk, kind, others],
            dst_ref=arrived.at[chunk, others],
            send_sem=send_sem.at[kind, chunk],
            recv_sem=recv_sem.at[kind, chunk],
            device_id=(pipe, partner),
            device_id_type=MESH,
        )

    def spread(chunk, kind, step, j, rows):
        rows = rows.astype(jnp.bfloat16)
        for k in range(local_experts):
            outbound[chunk, kind, k * split + j] = rows[k * cap:(k + 1) * cap]
        for turn in range(local_experts):
            k = lax.rem(seat // split + local_experts - 1 - turn, local_experts)
            if step == 0 and turn == local_experts - 1:
                local(chunk, kind).start()
            else:
                block(chunk, kind, k * split + j).start()

    def slab_cols(chunk, j):
        return pl.ds(pl.multiple_of(j * slab + chunk * LANE, LANE), LANE)

    def packed_copy(chunk, j):
        return pltpu.make_async_remote_copy(
            src_ref=packed.at[chunk, j], dst_ref=packed_in.at[chunk, j],
            send_sem=pack_send.at[chunk], recv_sem=pack_recv.at[chunk],
            device_id=(pipe, partner), device_id_type=MESH,
        )

    def packed_all(chunk):
        return pltpu.make_async_remote_copy(
            src_ref=packed.at[chunk], dst_ref=packed_in.at[chunk],
            send_sem=pack_send.at[chunk], recv_sem=pack_recv.at[chunk],
            device_id=(pipe, partner), device_id_type=MESH,
        )

    def slab_step(step, new, passed):
        j = lax.rem(seat + step, split)
        if passed is not None:
            rows = jnp.dot(expand[...], packed_in[passed, j], preferred_element_type=jnp.float32)
            spread(passed, 1, step, j, rows)
        if new is not None:
            rows = jnp.dot(place[...], grad[:, slab_cols(new, j)], preferred_element_type=jnp.float32)
            spread(new, 0, step, j, rows)
            rows = jnp.dot(pack[...], grad[:, slab_cols(new, j)], preferred_element_type=jnp.float32)
            packed[new, j] = rows.astype(jnp.bfloat16)
            packed_copy(new, j).start()

    def first_sends(chunk, carry):
        for step in range(split):
            slab_step(step, chunk, None)
        return carry

    first_sends(0, 0)
    load_hidden(0).start()
    load_hidden(1).start()
    for load in load_state:
        load.start()
    lax.fori_loop(1, plane, tell_plane, 0)
    lax.fori_loop(1, FIRST, first_sends, 0)

    send_routes.wait_recv()
    their_places, their_ranks, _ = one_hots(routes_in[...], side)
    expand[...] = lax.dot_general(
        their_places, their_ranks, (((1,), (1,)), ((), ())), preferred_element_type=jnp.float32
    ).astype(jnp.bfloat16)

    turns = expert_count // group

    def flip_turn(turn, carry):
        load_hidden(turn).wait()

        def flip(i, carry):
            at = pl.multiple_of((turn * group + i) * cap, cap)
            hidden_t[:, pl.ds(at, cap)] = hidden[turn % 2, i].T
            return carry

        lax.fori_loop(0, group, flip, 0)

        @pl.when(turn + 2 < turns)
        def _():
            load_hidden(turn + 2).start()

        return carry

    def code_copy(chunk):
        return pltpu.make_async_remote_copy(
            src_ref=code.at[chunk], dst_ref=code_in.at[chunk],
            send_sem=code_send.at[chunk], recv_sem=code_recv.at[chunk],
            device_id=(mirror, me), device_id_type=MESH,
        )

    def scale_copy(chunk):
        return pltpu.make_async_remote_copy(
            src_ref=scale.at[chunk], dst_ref=scale_in.at[chunk],
            send_sem=scale_send.at[chunk], recv_sem=scale_recv.at[chunk],
            device_id=(mirror, me), device_id_type=MESH,
        )

    def multiply(chunk, first, into):
        def one(i, carry):
            row = pl.multiple_of(i * tile, tile)
            rows = pl.ds(pl.multiple_of(first + row, tile), tile)
            cols = arrived[chunk].reshape(expert_count * cap, LANE)
            into[pl.ds(row, tile), :] = jnp.dot(hidden_t[rows, :], cols, preferred_element_type=jnp.float32)
            return carry

        lax.fori_loop(0, half // tile, one, 0)

    def finish(chunk):
        cols = pl.ds(pl.multiple_of(chunk * LANE, LANE), LANE)
        for part in range(half // tile):
            index = chunk * (half // tile) + part
            code_copy(index).wait_recv()
            scale_copy(index).wait_recv()
            rows = slice(part * tile, (part + 1) * tile)
            summed = own[chunk, rows] + code_in[index].astype(jnp.float32) * scale_in[index, 0:1, :]
            new_moment1 = 0.9 * moment1[rows, cols] + 0.1 * summed
            new_moment2 = 0.95 * moment2[rows, cols] + 0.05 * summed * summed
            weight = master[rows, cols]
            update = new_moment1 / (1.0 - 0.9**10) / (jnp.sqrt(new_moment2 / (1.0 - 0.95**10)) + 1e-08)
            master[rows, cols] = weight - 0.2 * (update + 0.05 * weight)
            moment1[rows, cols] = new_moment1
            moment2[rows, cols] = new_moment2

    def work(chunk, carry):
        for kind in range(2):
            all_blocks(chunk, kind).wait_recv()
            local(chunk, kind).wait()
        for part in range(half // tile):
            index = chunk * (half // tile) + part
            rows = pl.ds(pl.multiple_of(other_start + part * tile, tile), tile)
            other[...] = jnp.dot(
                hidden_t[rows, :], arrived[chunk].reshape(expert_count * cap, LANE), preferred_element_type=jnp.float32
            )
            value = other[...]
            top = jnp.maximum(jnp.max(jnp.abs(value), axis=0, keepdims=True), 1e-30)
            code[index] = jnp.floor(value * (32766.0 / top) + 0.5).astype(jnp.int16)
            scale[index] = jnp.broadcast_to(top * (1.0 / 32766.0), scale.shape[1:])
            code_copy(index).start()
            scale_copy(index).start()
        multiply(chunk, own_start, own.at[chunk])

        @pl.when(chunk >= LAG)
        def _():
            finish(chunk - LAG)

        return carry

    for load in load_state:
        load.wait()

    def both(chunk, carry):
        packed_all(chunk).wait_recv()
        for step in range(split):
            slab_step(step, chunk + FIRST, chunk)

        @pl.when(chunk < BEHIND)
        def _():
            lax.fori_loop(chunk * turns // BEHIND, (chunk + 1) * turns // BEHIND, flip_turn, 0)

        @pl.when(chunk >= BEHIND)
        def _():
            work(chunk - BEHIND, 0)

        return carry

    def passing(chunk, carry):
        packed_all(chunk).wait_recv()
        for step in range(split):
            slab_step(step, None, chunk)
        work(chunk - BEHIND, 0)
        return carry

    lax.fori_loop(0, chunks - FIRST, both, 0)

    over_all_plane.wait_recv()
    over_pair[0] = jnp.max(over_plane[...], axis=0)
    over_to_partner.start()

    lax.fori_loop(chunks - FIRST, chunks, passing, 0)

    over_to_partner.wait_recv()
    over_pipe[pipe] = jnp.maximum(over_pair[0], over_pair[1])
    for copy in over_to_pipes:
        copy.start()

    lax.fori_loop(chunks - BEHIND, chunks, work, 0)

    def finish_rest(chunk, carry):
        finish(chunk)
        return carry

    lax.fori_loop(chunks - LAG, chunks, finish_rest, 0)

    over_all_pipes.wait_recv()
    over_out[...] = jnp.max(over_pipe[...], axis=0)[0:1, 0:1]
    send_routes.wait_send()
    over_all_plane.wait_send()
    over_to_partner.wait_send()
    over_all_pipes.wait_send()

    def drain(chunk, carry):
        for kind in range(2):
            all_blocks(chunk, kind).wait_send()
        packed_all(chunk).wait_send()
        for part in range(half // tile):
            code_copy(chunk * (half // tile) + part).wait_send()
            scale_copy(chunk * (half // tile) + part).wait_send()
        return carry

    lax.fori_loop(0, chunks, drain, 0)


def store_kernel(*refs):
    count = len(refs) // 2
    sems = refs[-1]
    copies = [
        pltpu.make_async_copy(refs[i], refs[count + i].at[0, 0], sems.at[i]) for i in range(count)
    ]
    for copy in copies:
        copy.start()
    for copy in copies:
        copy.wait()


def body(out_grad, routes, saved_hidden, master, moment1, moment2):
    expert_count = lax.axis_size("expert")
    slots, width = out_grad.shape
    cap, hid = saved_hidden.shape[3:]
    half, cols = master.shape[2:]
    chunks = cols // LANE
    bf16, f32 = jnp.bfloat16, jnp.float32
    dma = pltpu.SemaphoreType.DMA
    split, plane = expert_count // EXPG, expert_count // 2
    state = pltpu.VMEM((half, cols), f32)
    operands = (
        out_grad, pltpu.with_memory_space_constraint(routes.reshape(1, slots), pltpu.HBM), saved_hidden,
        master, moment1, moment2,
    )

    def every_row():
        states = pl.pallas_call(
            exchange_kernel,
            out_shape=(state, state, state),
            in_specs=[
                pl.BlockSpec(memory_space=pl.ANY),
                pl.BlockSpec(memory_space=pltpu.HBM),
                pl.BlockSpec(memory_space=pl.ANY),
                pl.BlockSpec(memory_space=pl.ANY),
                pl.BlockSpec(memory_space=pl.ANY),
                pl.BlockSpec(memory_space=pl.ANY),
            ],
            out_specs=[pl.BlockSpec(memory_space=pltpu.VMEM)] * 3,
            scratch_shapes=[
                pltpu.VMEM((slots, width), bf16),
                pltpu.VMEM((1, slots), jnp.int32),
                pltpu.VMEM((EXPG * cap, slots), bf16),
                pltpu.VMEM((chunks, expert_count, cap, LANE), bf16),
                pltpu.VMEM((chunks, expert_count, cap, LANE), bf16),
                pltpu.VMEM((expert_count, cap, hid), bf16),
                pltpu.VMEM((hid, expert_count * cap), bf16),
                pltpu.VMEM((chunks, half, LANE), f32),
                pltpu.VMEM((half, LANE), f32),
                pltpu.VMEM((chunks, half, LANE), jnp.int16),
                pltpu.VMEM((chunks, half, LANE), jnp.int16),
                pltpu.VMEM((chunks, 8, LANE), f32),
                pltpu.VMEM((chunks, 8, LANE), f32),
                dma((6,)),
            ] + [dma((chunks,))] * 7,
            compiler_params=pltpu.CompilerParams(
                collective_id=1, has_side_effects=True, vmem_limit_bytes=48 * 1024 * 1024
            ),
            cost_estimate=pl.CostEstimate(
                flops=2 * expert_count * cap * hid * cols, bytes_accessed=16 << 20, transcendentals=0
            ),
            name="exchange",
        )(*operands)
        return stored(states)

    def stored(states):
        shape = jax.ShapeDtypeStruct((1, 1, half, cols), f32)
        return pl.pallas_call(
            store_kernel,
            out_shape=(shape, shape, shape),
            in_specs=[pl.BlockSpec(memory_space=pltpu.VMEM)] * 3,
            out_specs=[pl.BlockSpec(memory_space=pl.ANY)] * 3,
            scratch_shapes=[dma((3,))],
            compiler_params=pltpu.CompilerParams(vmem_limit_bytes=1024 * 1024),
            name="store",
        )(*(pltpu.with_memory_space_constraint(new, pltpu.VMEM) for new in states))

    *states, over = pl.pallas_call(
        relay_kernel,
        out_shape=(state, state, state, jax.ShapeDtypeStruct((1, 1), jnp.int32)),
        in_specs=[pl.BlockSpec(memory_space=pl.ANY), pl.BlockSpec(memory_space=pltpu.HBM)]
        + [pl.BlockSpec(memory_space=pl.ANY)] * 4,
        out_specs=[pl.BlockSpec(memory_space=pltpu.VMEM)] * 4,
        scratch_shapes=[
            pltpu.VMEM((slots, width), bf16),
            pltpu.VMEM((1, slots), jnp.int32),
            pltpu.VMEM((1, slots), jnp.int32),
            pltpu.VMEM((EXPG // 2 * cap, slots), bf16),
            pltpu.VMEM((CROSSING, slots), bf16),
            pltpu.VMEM((EXPG // 2 * cap, CROSSING), bf16),
            pltpu.VMEM((chunks, split, CROSSING, LANE), bf16),
            pltpu.VMEM((chunks, split, CROSSING, LANE), bf16),
            pltpu.VMEM((chunks, 2, plane, cap, LANE), bf16),
            pltpu.VMEM((chunks, expert_count, cap, LANE), bf16),
            pltpu.VMEM((2, expert_count // 8, cap, hid), bf16),
            pltpu.VMEM((hid, expert_count * cap), bf16),
            pltpu.VMEM((chunks, half, LANE), f32),
            pltpu.VMEM((half // 2, LANE), f32),
            pltpu.VMEM((2 * chunks, half // 2, LANE), jnp.int16),
            pltpu.VMEM((2 * chunks, half // 2, LANE), jnp.int16),
            pltpu.VMEM((2 * chunks, 8, LANE), f32),
            pltpu.VMEM((2 * chunks, 8, LANE), f32),
            pltpu.VMEM((plane, 8, LANE), jnp.int32),
            pltpu.VMEM((2, 8, LANE), jnp.int32),
            pltpu.VMEM((lax.axis_size("pipe"), 8, LANE), jnp.int32),
            dma((5,)),
            dma((2,)),
            dma((2,)),
            dma((6,)),
            dma((chunks,)),
            dma((chunks,)),
            dma((2, chunks)),
            dma((2, chunks)),
            dma((2, chunks)),
        ] + [dma((2 * chunks,))] * 4,
        compiler_params=pltpu.CompilerParams(
            collective_id=0, has_side_effects=True, vmem_limit_bytes=48 * 1024 * 1024
        ),
        cost_estimate=pl.CostEstimate(
            flops=2 * expert_count * cap * hid * cols, bytes_accessed=16 << 20, transcendentals=0
        ),
        name="relay",
    )(*operands)
    done = stored(states)
    return lax.cond(over[0, 0] > 0, every_row, lambda: done)


def solution(mesh):
    in_specs = (
        P(("pipe", "expert"), None),
        P(("pipe", "expert"), None),
        P("pipe", "expert", None, None, None),
        P("pipe", "expert", None, None),
        P("pipe", "expert", None, None),
        P("pipe", "expert", None, None),
    )
    out_specs = (
        P("pipe", "expert", None, None),
        P("pipe", "expert", None, None),
        P("pipe", "expert", None, None),
    )
    return jax.shard_map(body, mesh=mesh, in_specs=in_specs, out_specs=out_specs, check_vma=False)
```

```python
import jax
import jax.numpy as jnp
from jax import lax
from jax.experimental import pallas as pl
from jax.experimental.pallas import tpu as pltpu
from jax.sharding import PartitionSpec as P

EXPG = 4
LANE = 128
LAG = 3
FIRST = 5
BEHIND = 2
CROSSING = 208
MESH = pl.DeviceIdType.MESH


def exchange_kernel(
    grad_hbm, routes_hbm, hidden_hbm, master_hbm, moment1_hbm, moment2_hbm, master, moment1, moment2,
    grad, routes, place, outbound, arrived, hidden, hidden_t, own, other, code, code_in, scale, scale_in,
    load_sem, local_sem, send_sem, recv_sem, code_send, code_recv, scale_send, scale_recv,
):
    pipe, me = lax.axis_index("pipe"), lax.axis_index("expert")
    pipe_count, expert_count = lax.axis_size("pipe"), lax.axis_size("expert")
    chunks, _, cap, _ = outbound.shape
    slots, width = grad.shape
    split = expert_count // EXPG
    slab = width // split
    hid = hidden_t.shape[0]
    half = hid // 2
    mirror = pipe_count - 1 - pipe
    keep_high = pipe // (pipe_count // 2)
    own_start = pl.multiple_of(keep_high * half, half)
    other_start = pl.multiple_of((1 - keep_high) * half, half)
    tile = half // 2

    load_grad = pltpu.make_async_copy(grad_hbm, grad, load_sem.at[0])
    load_grad.start()
    load_routes = pltpu.make_async_copy(routes_hbm, routes, load_sem.at[5])
    load_routes.start()
    load_hidden = pltpu.make_async_copy(hidden_hbm.at[0, 0], hidden, load_sem.at[1])
    load_hidden.start()
    load_state = [
        pltpu.make_async_copy(src.at[0, 0], dst, load_sem.at[2 + i])
        for i, (src, dst) in enumerate(((master_hbm, master), (moment1_hbm, moment1), (moment2_hbm, moment2)))
    ]
    for load in load_state:
        load.start()

    barrier = pltpu.get_barrier_semaphore()

    def greet(step, carry):
        pl.semaphore_signal(
            barrier, inc=1, device_id=(pipe, lax.rem(me + step, expert_count)), device_id_type=MESH
        )
        return carry

    lax.fori_loop(1, expert_count, greet, 0)
    pl.semaphore_signal(barrier, inc=1, device_id=(mirror, me), device_id_type=MESH)

    load_routes.wait()
    route = routes[...]
    chosen = jnp.broadcast_to(route, (8, slots)) == lax.broadcasted_iota(jnp.int32, (8, slots), 0)
    earlier = lax.broadcasted_iota(jnp.int32, (slots, slots), 0) < lax.broadcasted_iota(jnp.int32, (slots, slots), 1)
    before = jnp.dot(
        chosen.astype(jnp.bfloat16), earlier.astype(jnp.bfloat16), preferred_element_type=jnp.float32
    )
    rank = jnp.sum(jnp.where(chosen, before, 0.0), axis=0, keepdims=True).astype(jnp.int32)
    flat = jnp.broadcast_to(route * cap + rank, (EXPG * cap, slots))
    placed = flat == lax.broadcasted_iota(jnp.int32, (EXPG * cap, slots), 0)
    place[...] = placed.astype(jnp.bfloat16)

    load_grad.wait()

    def block(chunk, peer):
        return pltpu.make_async_remote_copy(
            src_ref=outbound.at[chunk, peer],
            dst_ref=arrived.at[chunk, me],
            send_sem=send_sem.at[chunk],
            recv_sem=recv_sem.at[chunk],
            device_id=(pipe, peer),
            device_id_type=MESH,
        )

    def local(chunk):
        return pltpu.make_async_copy(outbound.at[chunk, me], arrived.at[chunk, me], local_sem.at[chunk])

    def pick_send(chunk, carry):
        for step in range(split):
            j = lax.rem(me + step, split)
            start = pl.multiple_of(j * slab + chunk * LANE, LANE)
            picked = jnp.dot(place[...], grad[:, pl.ds(start, LANE)], preferred_element_type=jnp.float32)
            picked = picked.astype(jnp.bfloat16)
            for k in range(EXPG):
                outbound[chunk, k * split + j] = picked[k * cap:(k + 1) * cap]
            for turn_k in range(EXPG):
                k = lax.rem(me // split + EXPG - 1 - turn_k, EXPG)
                if step == 0 and turn_k == EXPG - 1:
                    local(chunk).start()
                else:
                    block(chunk, k * split + j).start()
        return carry

    def all_blocks(chunk):
        others = pl.ds(0, expert_count - 1)
        return pltpu.make_async_remote_copy(
            src_ref=outbound.at[chunk, others],
            dst_ref=arrived.at[chunk, others],
            send_sem=send_sem.at[chunk],
            recv_sem=recv_sem.at[chunk],
            device_id=(pipe, me),
            device_id_type=MESH,
        )

    pl.semaphore_wait(barrier, expert_count)
    lax.fori_loop(0, chunks, pick_send, 0)

    load_hidden.wait()

    def turn(s, carry):
        at = pl.multiple_of(s * cap, cap)
        hidden_t[:, pl.ds(at, cap)] = hidden[s].T
        return carry

    lax.fori_loop(0, expert_count, turn, 0)

    def code_copy(chunk):
        return pltpu.make_async_remote_copy(
            src_ref=code.at[chunk], dst_ref=code_in.at[chunk],
            send_sem=code_send.at[chunk], recv_sem=code_recv.at[chunk],
            device_id=(mirror, me), device_id_type=MESH,
        )

    def scale_copy(chunk):
        return pltpu.make_async_remote_copy(
            src_ref=scale.at[chunk], dst_ref=scale_in.at[chunk],
            send_sem=scale_send.at[chunk], recv_sem=scale_recv.at[chunk],
            device_id=(mirror, me), device_id_type=MESH,
        )

    def multiply(chunk, first, into):
        def one(i, carry):
            row = pl.multiple_of(i * tile, tile)
            rows = pl.ds(pl.multiple_of(first + row, tile), tile)
            cols = arrived[chunk].reshape(expert_count * cap, LANE)
            into[pl.ds(row, tile), :] = jnp.dot(hidden_t[rows, :], cols, preferred_element_type=jnp.float32)
            return carry

        lax.fori_loop(0, half // tile, one, 0)

    def finish(chunk):
        code_copy(chunk).wait_recv()
        scale_copy(chunk).wait_recv()
        summed = own[chunk] + code_in[chunk].astype(jnp.float32) * scale_in[chunk, 0:1, :]
        cols = pl.ds(pl.multiple_of(chunk * LANE, LANE), LANE)
        new_moment1 = 0.9 * moment1[:, cols] + 0.1 * summed
        new_moment2 = 0.95 * moment2[:, cols] + 0.05 * summed * summed
        weight = master[:, cols]
        update = new_moment1 / (1.0 - 0.9**10) / (jnp.sqrt(new_moment2 / (1.0 - 0.95**10)) + 1e-08)
        master[:, cols] = weight - 0.2 * (update + 0.05 * weight)
        moment1[:, cols] = new_moment1
        moment2[:, cols] = new_moment2

    def work(chunk, carry):
        all_blocks(chunk).wait_recv()
        local(chunk).wait()
        multiply(chunk, other_start, other)
        part = other[...]
        top = jnp.maximum(jnp.max(jnp.abs(part), axis=0, keepdims=True), 1e-30)
        code[chunk] = jnp.floor(part * (32766.0 / top) + 0.5).astype(jnp.int16)
        scale[chunk] = jnp.broadcast_to(top * (1.0 / 32766.0), scale.shape[1:])
        code_copy(chunk).start()
        scale_copy(chunk).start()
        multiply(chunk, own_start, own.at[chunk])

        @pl.when(chunk >= LAG)
        def _():
            finish(chunk - LAG)

        return carry

    for load in load_state:
        load.wait()
    lax.fori_loop(0, chunks, work, 0)

    def finish_rest(chunk, carry):
        finish(chunk)
        return carry

    lax.fori_loop(chunks - LAG, chunks, finish_rest, 0)

    def drain(chunk, carry):
        all_blocks(chunk).wait_send()
        code_copy(chunk).wait_send()
        scale_copy(chunk).wait_send()
        return carry

    lax.fori_loop(0, chunks, drain, 0)


def relay_kernel(
    grad_hbm, routes_hbm, hidden_hbm, master_hbm, moment1_hbm, moment2_hbm, master, moment1, moment2, over_out,
    grad, routes, routes_in, place, pack, expand, packed, packed_in, outbound, arrived, hidden, hidden_t,
    own, other, code, code_in, scale, scale_in, over_plane, over_pair, over_pipe,
    load_sem, hidden_sem, routes_sem, over_sem, pack_send, pack_recv, local_sem, send_sem, recv_sem,
    code_send, code_recv, scale_send, scale_recv,
):
    pipe, me = lax.axis_index("pipe"), lax.axis_index("expert")
    pipe_count, expert_count = lax.axis_size("pipe"), lax.axis_size("expert")
    chunks, _, plane, cap, _ = outbound.shape
    slots, width = grad.shape
    split = expert_count // EXPG
    slab = width // split
    hid = hidden_t.shape[0]
    half = hid // 2
    mirror = pipe_count - 1 - pipe
    keep_high = pipe // (pipe_count // 2)
    own_start = pl.multiple_of(keep_high * half, half)
    other_start = pl.multiple_of((1 - keep_high) * half, half)
    tile = half // 2
    side = me // plane
    seat = me % plane
    base = side * plane
    partner = lax.rem(me + plane, expert_count)
    local_experts = EXPG // 2
    bound = packed.shape[2]

    load_routes = pltpu.make_async_copy(routes_hbm, routes, load_sem.at[0])
    load_routes.start()
    load_grad = pltpu.make_async_copy(grad_hbm, grad, load_sem.at[1])
    load_grad.start()
    group = hidden.shape[1]

    def load_hidden(turn):
        return pltpu.make_async_copy(
            hidden_hbm.at[0, 0, pl.ds(turn * group, group)], hidden.at[turn % 2], hidden_sem.at[turn % 2]
        )

    load_state = [
        pltpu.make_async_copy(src.at[0, 0], dst, load_sem.at[2 + i])
        for i, (src, dst) in enumerate(((master_hbm, master), (moment1_hbm, moment1), (moment2_hbm, moment2)))
    ]

    barrier = pltpu.get_barrier_semaphore()

    def greet(step, carry):
        pl.semaphore_signal(
            barrier, inc=1, device_id=(pipe, base + lax.rem(seat + step, plane)), device_id_type=MESH
        )
        return carry

    lax.fori_loop(1, plane, greet, 0)
    pl.semaphore_signal(barrier, inc=1, device_id=(pipe, partner), device_id_type=MESH)
    for step in range(1, pipe_count):
        pl.semaphore_signal(barrier, inc=1, device_id=(lax.rem(pipe + step, pipe_count), me), device_id_type=MESH)

    def one_hots(route, packed_side):
        expert = lax.broadcasted_iota(jnp.int32, (8, slots), 0)
        chosen = jnp.broadcast_to(route, (8, slots)) == expert
        earlier = lax.broadcasted_iota(jnp.int32, (slots, slots), 0) < lax.broadcasted_iota(jnp.int32, (slots, slots), 1)
        before = jnp.dot(
            chosen.astype(jnp.bfloat16), earlier.astype(jnp.bfloat16), preferred_element_type=jnp.float32
        )
        rank = jnp.sum(jnp.where(chosen, before, 0.0), axis=0, keepdims=True).astype(jnp.int32)
        flat = jnp.broadcast_to((route - side * local_experts) * cap + rank, (local_experts * cap, slots))
        places = flat == lax.broadcasted_iota(jnp.int32, (local_experts * cap, slots), 0)
        first = packed_side * local_experts
        in_side = (expert >= first) & (expert < first + local_experts)
        order = jnp.sum(jnp.where(in_side, before, 0.0), axis=0, keepdims=True).astype(jnp.int32)
        goes = (route >= first) & (route < first + local_experts)
        order = jnp.broadcast_to(jnp.where(goes, order, -1), (bound, slots))
        ranks = order == lax.broadcasted_iota(jnp.int32, (bound, slots), 0)
        return places.astype(jnp.bfloat16), ranks.astype(jnp.bfloat16), goes

    load_routes.wait()
    own_places, own_ranks, goes = one_hots(routes[...], 1 - side)
    place[...] = own_places
    pack[...] = own_ranks
    crossing = jnp.sum(goes.astype(jnp.float32), axis=1, keepdims=True)
    over = jnp.broadcast_to((crossing > bound).astype(jnp.int32), over_pair.shape[1:])
    over_plane[seat] = over

    load_grad.wait()
    pl.semaphore_wait(barrier, plane - 1 + 1 + pipe_count - 1)

    send_routes = pltpu.make_async_remote_copy(
        src_ref=routes, dst_ref=routes_in, send_sem=routes_sem.at[0], recv_sem=routes_sem.at[1],
        device_id=(pipe, partner), device_id_type=MESH,
    )
    send_routes.start()

    def over_to_plane(seat_to):
        return pltpu.make_async_remote_copy(
            src_ref=over_plane.at[seat], dst_ref=over_plane.at[seat],
            send_sem=over_sem.at[0], recv_sem=over_sem.at[1],
            device_id=(pipe, base + seat_to), device_id_type=MESH,
        )

    def tell_plane(step, carry):
        over_to_plane(lax.rem(seat + step, plane)).start()
        return carry

    over_all_plane = pltpu.make_async_remote_copy(
        src_ref=over_plane.at[pl.ds(0, plane - 1)], dst_ref=over_plane.at[pl.ds(0, plane - 1)],
        send_sem=over_sem.at[0], recv_sem=over_sem.at[1],
        device_id=(pipe, partner), device_id_type=MESH,
    )
    over_to_partner = pltpu.make_async_remote_copy(
        src_ref=over_pair.at[0], dst_ref=over_pair.at[1],
        send_sem=over_sem.at[2], recv_sem=over_sem.at[3],
        device_id=(pipe, partner), device_id_type=MESH,
    )
    over_to_pipes = [
        pltpu.make_async_remote_copy(
            src_ref=over_pipe.at[pipe], dst_ref=over_pipe.at[pipe],
            send_sem=over_sem.at[4], recv_sem=over_sem.at[5],
            device_id=(lax.rem(pipe + step, pipe_count), me), device_id_type=MESH,
        )
        for step in range(1, pipe_count)
    ]
    over_all_pipes = pltpu.make_async_remote_copy(
        src_ref=over_pipe.at[pl.ds(0, pipe_count - 1)], dst_ref=over_pipe.at[pl.ds(0, pipe_count - 1)],
        send_sem=over_sem.at[4], recv_sem=over_sem.at[5],
        device_id=(mirror, me), device_id_type=MESH,
    )

    def block(chunk, kind, to):
        return pltpu.make_async_remote_copy(
            src_ref=outbound.at[chunk, kind, to],
            dst_ref=arrived.at[chunk, me if kind == 0 else partner],
            send_sem=send_sem.at[kind, chunk],
            recv_sem=recv_sem.at[kind, chunk],
            device_id=(pipe, base + to),
            device_id_type=MESH,
        )

    def local(chunk, kind):
        return pltpu.make_async_copy(
            outbound.at[chunk, kind, seat],
            arrived.at[chunk, me if kind == 0 else partner],
            local_sem.at[kind, chunk],
        )

    def all_blocks(chunk, kind):
        others = pl.ds(0, plane - 1)
        return pltpu.make_async_remote_copy(
            src_ref=outbound.at[chunk, kind, others],
            dst_ref=arrived.at[chunk, others],
            send_sem=send_sem.at[kind, chunk],
            recv_sem=recv_sem.at[kind, chunk],
            device_id=(pipe, partner),
            device_id_type=MESH,
        )

    def spread(chunk, kind, step, j, rows):
        rows = rows.astype(jnp.bfloat16)
        for k in range(local_experts):
            outbound[chunk, kind, k * split + j] = rows[k * cap:(k + 1) * cap]
        for turn in range(local_experts):
            k = lax.rem(seat // split + local_experts - 1 - turn, local_experts)
            if step == 0 and turn == local_experts - 1:
                local(chunk, kind).start()
            else:
                block(chunk, kind, k * split + j).start()

    def slab_cols(chunk, j):
        return pl.ds(pl.multiple_of(j * slab + chunk * LANE, LANE), LANE)

    def packed_copy(chunk, j):
        return pltpu.make_async_remote_copy(
            src_ref=packed.at[chunk, j], dst_ref=packed_in.at[chunk, j],
            send_sem=pack_send.at[chunk], recv_sem=pack_recv.at[chunk],
            device_id=(pipe, partner), device_id_type=MESH,
        )

    def packed_all(chunk):
        return pltpu.make_async_remote_copy(
            src_ref=packed.at[chunk], dst_ref=packed_in.at[chunk],
            send_sem=pack_send.at[chunk], recv_sem=pack_recv.at[chunk],
            device_id=(pipe, partner), device_id_type=MESH,
        )

    def slab_step(step, new, passed):
        j = lax.rem(seat + step, split)
        if passed is not None:
            far = lax.rem(seat + split - step, split)
            rows = jnp.dot(expand[...], packed_in[passed, far], preferred_element_type=jnp.float32)
            spread(passed, 1, step, far, rows)
        if new is not None:
            rows = jnp.dot(place[...], grad[:, slab_cols(new, j)], preferred_element_type=jnp.float32)
            spread(new, 0, step, j, rows)
            rows = jnp.dot(pack[...], grad[:, slab_cols(new, j)], preferred_element_type=jnp.float32)
            packed[new, j] = rows.astype(jnp.bfloat16)
            packed_copy(new, j).start()

    def first_sends(chunk, carry):
        for step in range(split):
            slab_step(step, chunk, None)
        return carry

    first_sends(0, 0)
    load_hidden(0).start()
    load_hidden(1).start()
    for load in load_state:
        load.start()
    lax.fori_loop(1, plane, tell_plane, 0)
    lax.fori_loop(1, FIRST, first_sends, 0)

    send_routes.wait_recv()
    their_places, their_ranks, _ = one_hots(routes_in[...], side)
    expand[...] = lax.dot_general(
        their_places, their_ranks, (((1,), (1,)), ((), ())), preferred_element_type=jnp.float32
    ).astype(jnp.bfloat16)

    turns = expert_count // group

    def flip_turn(turn, carry):
        load_hidden(turn).wait()

        def flip(i, carry):
            at = pl.multiple_of((turn * group + i) * cap, cap)
            hidden_t[:, pl.ds(at, cap)] = hidden[turn % 2, i].T
            return carry

        lax.fori_loop(0, group, flip, 0)

        @pl.when(turn + 2 < turns)
        def _():
            load_hidden(turn + 2).start()

        return carry

    def code_copy(chunk):
        return pltpu.make_async_remote_copy(
            src_ref=code.at[chunk], dst_ref=code_in.at[chunk],
            send_sem=code_send.at[chunk], recv_sem=code_recv.at[chunk],
            device_id=(mirror, me), device_id_type=MESH,
        )

    def scale_copy(chunk):
        return pltpu.make_async_remote_copy(
            src_ref=scale.at[chunk], dst_ref=scale_in.at[chunk],
            send_sem=scale_send.at[chunk], recv_sem=scale_recv.at[chunk],
            device_id=(mirror, me), device_id_type=MESH,
        )

    def multiply(chunk, first, into):
        def one(i, carry):
            row = pl.multiple_of(i * tile, tile)
            rows = pl.ds(pl.multiple_of(first + row, tile), tile)
            cols = arrived[chunk].reshape(expert_count * cap, LANE)
            into[pl.ds(row, tile), :] = jnp.dot(hidden_t[rows, :], cols, preferred_element_type=jnp.float32)
            return carry

        lax.fori_loop(0, half // tile, one, 0)

    def finish(chunk):
        cols = pl.ds(pl.multiple_of(chunk * LANE, LANE), LANE)
        for part in range(half // tile):
            index = chunk * (half // tile) + part
            code_copy(index).wait_recv()
            scale_copy(index).wait_recv()
            rows = slice(part * tile, (part + 1) * tile)
            summed = own[chunk, rows] + code_in[index].astype(jnp.float32) * scale_in[index, 0:1, :]
            new_moment1 = 0.9 * moment1[rows, cols] + 0.1 * summed
            new_moment2 = 0.95 * moment2[rows, cols] + 0.05 * summed * summed
            weight = master[rows, cols]
            update = new_moment1 / (1.0 - 0.9**10) / (jnp.sqrt(new_moment2 / (1.0 - 0.95**10)) + 1e-08)
            master[rows, cols] = weight - 0.2 * (update + 0.05 * weight)
            moment1[rows, cols] = new_moment1
            moment2[rows, cols] = new_moment2

    def work(chunk, carry):
        for kind in range(2):
            all_blocks(chunk, kind).wait_recv()
            local(chunk, kind).wait()
        for part in range(half // tile):
            index = chunk * (half // tile) + part
            rows = pl.ds(pl.multiple_of(other_start + part * tile, tile), tile)
            other[...] = jnp.dot(
                hidden_t[rows, :], arrived[chunk].reshape(expert_count * cap, LANE), preferred_element_type=jnp.float32
            )
            value = other[...]
            top = jnp.maximum(jnp.max(jnp.abs(value), axis=0, keepdims=True), 1e-30)
            code[index] = jnp.floor(value * (32766.0 / top) + 0.5).astype(jnp.int16)
            scale[index] = jnp.broadcast_to(top * (1.0 / 32766.0), scale.shape[1:])
            code_copy(index).start()
            scale_copy(index).start()
        multiply(chunk, own_start, own.at[chunk])

        @pl.when(chunk >= LAG)
        def _():
            finish(chunk - LAG)

        return carry

    for load in load_state:
        load.wait()

    def both(chunk, carry):
        packed_all(chunk).wait_recv()
        for step in range(split):
            slab_step(step, chunk + FIRST, chunk)

        @pl.when(chunk < BEHIND)
        def _():
            lax.fori_loop(chunk * turns // BEHIND, (chunk + 1) * turns // BEHIND, flip_turn, 0)

        @pl.when(chunk >= BEHIND)
        def _():
            work(chunk - BEHIND, 0)

        return carry

    def passing(chunk, carry):
        packed_all(chunk).wait_recv()
        for step in range(split):
            slab_step(step, None, chunk)
        work(chunk - BEHIND, 0)
        return carry

    lax.fori_loop(0, chunks - FIRST, both, 0)

    over_all_plane.wait_recv()
    over_pair[0] = jnp.max(over_plane[...], axis=0)
    over_to_partner.start()

    lax.fori_loop(chunks - FIRST, chunks, passing, 0)

    over_to_partner.wait_recv()
    over_pipe[pipe] = jnp.maximum(over_pair[0], over_pair[1])
    for copy in over_to_pipes:
        copy.start()

    lax.fori_loop(chunks - BEHIND, chunks, work, 0)

    def finish_rest(chunk, carry):
        finish(chunk)
        return carry

    lax.fori_loop(chunks - LAG, chunks, finish_rest, 0)

    over_all_pipes.wait_recv()
    over_out[...] = jnp.max(over_pipe[...], axis=0)[0:1, 0:1]
    send_routes.wait_send()
    over_all_plane.wait_send()
    over_to_partner.wait_send()
    over_all_pipes.wait_send()

    def drain(chunk, carry):
        for kind in range(2):
            all_blocks(chunk, kind).wait_send()
        packed_all(chunk).wait_send()
        for part in range(half // tile):
            code_copy(chunk * (half // tile) + part).wait_send()
            scale_copy(chunk * (half // tile) + part).wait_send()
        return carry

    lax.fori_loop(0, chunks, drain, 0)


def store_kernel(*refs):
    count = len(refs) // 2
    sems = refs[-1]
    copies = [
        pltpu.make_async_copy(refs[i], refs[count + i].at[0, 0], sems.at[i]) for i in range(count)
    ]
    for copy in copies:
        copy.start()
    for copy in copies:
        copy.wait()


def body(out_grad, routes, saved_hidden, master, moment1, moment2):
    expert_count = lax.axis_size("expert")
    slots, width = out_grad.shape
    cap, hid = saved_hidden.shape[3:]
    half, cols = master.shape[2:]
    chunks = cols // LANE
    bf16, f32 = jnp.bfloat16, jnp.float32
    dma = pltpu.SemaphoreType.DMA
    split, plane = expert_count // EXPG, expert_count // 2
    state = pltpu.VMEM((half, cols), f32)
    operands = (
        out_grad, pltpu.with_memory_space_constraint(routes.reshape(1, slots), pltpu.HBM), saved_hidden,
        master, moment1, moment2,
    )

    def every_row():
        states = pl.pallas_call(
            exchange_kernel,
            out_shape=(state, state, state),
            in_specs=[
                pl.BlockSpec(memory_space=pl.ANY),
                pl.BlockSpec(memory_space=pltpu.HBM),
                pl.BlockSpec(memory_space=pl.ANY),
                pl.BlockSpec(memory_space=pl.ANY),
                pl.BlockSpec(memory_space=pl.ANY),
                pl.BlockSpec(memory_space=pl.ANY),
            ],
            out_specs=[pl.BlockSpec(memory_space=pltpu.VMEM)] * 3,
            scratch_shapes=[
                pltpu.VMEM((slots, width), bf16),
                pltpu.VMEM((1, slots), jnp.int32),
                pltpu.VMEM((EXPG * cap, slots), bf16),
                pltpu.VMEM((chunks, expert_count, cap, LANE), bf16),
                pltpu.VMEM((chunks, expert_count, cap, LANE), bf16),
                pltpu.VMEM((expert_count, cap, hid), bf16),
                pltpu.VMEM((hid, expert_count * cap), bf16),
                pltpu.VMEM((chunks, half, LANE), f32),
                pltpu.VMEM((half, LANE), f32),
                pltpu.VMEM((chunks, half, LANE), jnp.int16),
                pltpu.VMEM((chunks, half, LANE), jnp.int16),
                pltpu.VMEM((chunks, 8, LANE), f32),
                pltpu.VMEM((chunks, 8, LANE), f32),
                dma((6,)),
            ] + [dma((chunks,))] * 7,
            compiler_params=pltpu.CompilerParams(
                collective_id=1, has_side_effects=True, vmem_limit_bytes=48 * 1024 * 1024
            ),
            cost_estimate=pl.CostEstimate(
                flops=2 * expert_count * cap * hid * cols, bytes_accessed=16 << 20, transcendentals=0
            ),
            name="exchange",
        )(*operands)
        return stored(states)

    def stored(states):
        shape = jax.ShapeDtypeStruct((1, 1, half, cols), f32)
        return pl.pallas_call(
            store_kernel,
            out_shape=(shape, shape, shape),
            in_specs=[pl.BlockSpec(memory_space=pltpu.VMEM)] * 3,
            out_specs=[pl.BlockSpec(memory_space=pl.ANY)] * 3,
            scratch_shapes=[dma((3,))],
            compiler_params=pltpu.CompilerParams(vmem_limit_bytes=1024 * 1024),
            name="store",
        )(*(pltpu.with_memory_space_constraint(new, pltpu.VMEM) for new in states))

    *states, over = pl.pallas_call(
        relay_kernel,
        out_shape=(state, state, state, jax.ShapeDtypeStruct((1, 1), jnp.int32)),
        in_specs=[pl.BlockSpec(memory_space=pl.ANY), pl.BlockSpec(memory_space=pltpu.HBM)]
        + [pl.BlockSpec(memory_space=pl.ANY)] * 4,
        out_specs=[pl.BlockSpec(memory_space=pltpu.VMEM)] * 4,
        scratch_shapes=[
            pltpu.VMEM((slots, width), bf16),
            pltpu.VMEM((1, slots), jnp.int32),
            pltpu.VMEM((1, slots), jnp.int32),
            pltpu.VMEM((EXPG // 2 * cap, slots), bf16),
            pltpu.VMEM((CROSSING, slots), bf16),
            pltpu.VMEM((EXPG // 2 * cap, CROSSING), bf16),
            pltpu.VMEM((chunks, split, CROSSING, LANE), bf16),
            pltpu.VMEM((chunks, split, CROSSING, LANE), bf16),
            pltpu.VMEM((chunks, 2, plane, cap, LANE), bf16),
            pltpu.VMEM((chunks, expert_count, cap, LANE), bf16),
            pltpu.VMEM((2, expert_count // 8, cap, hid), bf16),
            pltpu.VMEM((hid, expert_count * cap), bf16),
            pltpu.VMEM((chunks, half, LANE), f32),
            pltpu.VMEM((half // 2, LANE), f32),
            pltpu.VMEM((2 * chunks, half // 2, LANE), jnp.int16),
            pltpu.VMEM((2 * chunks, half // 2, LANE), jnp.int16),
            pltpu.VMEM((2 * chunks, 8, LANE), f32),
            pltpu.VMEM((2 * chunks, 8, LANE), f32),
            pltpu.VMEM((plane, 8, LANE), jnp.int32),
            pltpu.VMEM((2, 8, LANE), jnp.int32),
            pltpu.VMEM((lax.axis_size("pipe"), 8, LANE), jnp.int32),
            dma((5,)),
            dma((2,)),
            dma((2,)),
            dma((6,)),
            dma((chunks,)),
            dma((chunks,)),
            dma((2, chunks)),
            dma((2, chunks)),
            dma((2, chunks)),
        ] + [dma((2 * chunks,))] * 4,
        compiler_params=pltpu.CompilerParams(
            collective_id=0, has_side_effects=True, vmem_limit_bytes=48 * 1024 * 1024
        ),
        cost_estimate=pl.CostEstimate(
            flops=2 * expert_count * cap * hid * cols, bytes_accessed=16 << 20, transcendentals=0
        ),
        name="relay",
    )(*operands)
    done = stored(states)
    return lax.cond(over[0, 0] > 0, every_row, lambda: done)


def solution(mesh):
    in_specs = (
        P(("pipe", "expert"), None),
        P(("pipe", "expert"), None),
        P("pipe", "expert", None, None, None),
        P("pipe", "expert", None, None),
        P("pipe", "expert", None, None),
        P("pipe", "expert", None, None),
    )
    out_specs = (
        P("pipe", "expert", None, None),
        P("pipe", "expert", None, None),
        P("pipe", "expert", None, None),
    )
    return jax.shard_map(body, mesh=mesh, in_specs=in_specs, out_specs=out_specs, check_vma=False)
```
